256 devices in a mesh: band: 4 (over z_hi), fft: 64 (over y, z_lo, x, core).
Axes of the slice: x: 4, y: 4, z: 8 (z_hi: 4, z_lo: 2; z = z_hi * 2 + z_lo), core: 2. Of those that a mesh axis runs over, the one named last changes fastest.
Arguments:
- psi: float32 [2, 4, 160, 16384], P(None, 'band', None, 'fft'), may hold values from -8 to 8
- potential: float32 [320, 320, 320], P('fft'), may hold values from -5 to 5
- stick_columns: int32 [16384], replicated, may hold values from 0 to 25599, as said below
Outputs:
- hpsi: float32 [2, 4, 160, 16384], P(None, 'band', None, 'fft')
- margin: float32 [2, 4, 4], P(None, None, 'band')
The draws below stay inside these ranges and needn't reach their ends.
Inputs may be any that keep to these rules, and one draw needn't show every extreme that they name: `stick_columns`: distinct values.
All inputs are finite; a program needn't handle non-finite values.
Results may differ from the reference program's by a relative error of at most 0.000077.
Values sent between devices are 32-bit elements; how exact they have to be, the bound alone decides.
A program may use at most 128 MiB of HBM per device.

```python
import math
import jax
import jax.numpy as jnp
from jax import lax

NG = 320
KB = 160
STICKS = 16384
BANDS = 4


def draw_stick_columns(key, part):
    key = jax.random.fold_in(key, 11)
    total = KB * KB
    order = jax.random.permutation(key, total).astype(jnp.int32)
    ranking = jnp.argsort(order).astype(jnp.int32)
    column = jnp.arange(total, dtype=jnp.int32)
    centre = KB // 2
    along_u = column // KB - centre
    along_v = column % KB - centre
    radius = along_u * along_u + along_v * along_v
    tier = jnp.where(radius < centre * centre, 1, 2)
    tier = jnp.where((column == 0) | (column == total - 1), 0, tier)
    priority = tier * total + ranking
    chosen = jnp.argsort(priority)[:STICKS]
    return chosen.astype(jnp.int32)


def draw_psi(key, part):
    key = jax.random.fold_in(key, 23)
    first, second, third = jax.random.split(key, 3)
    shape = (2, BANDS, KB, STICKS)
    own = jax.random.truncated_normal(first, -4.0, 4.0, shape, jnp.float32)
    common = jax.random.truncated_normal(second, -4.0, 4.0, (2, 1, KB, STICKS), jnp.float32)
    mixing = jax.random.uniform(third, (1, BANDS, 1, 1), jnp.float32, 0.3, 1.0)
    return own + mixing * common


def level_of(key, dims, cuts, low, top_value):
    factor_of, own = 1.0, jax.random.fold_in(key, 6)
    for position, shards_of in cuts:
        draws = jnp.exp(jax.random.uniform(jax.random.fold_in(own, position), (shards_of,), jnp.float32, low / len(cuts), top_value / len(cuts)))
        factor_of = factor_of * jnp.repeat(draws, dims[position] // shards_of).reshape([-1 if axis == position else 1 for axis in range(len(dims))])
    return factor_of


def centred(rng, extent, spread, limit, cuts=(), kind=jnp.bfloat16):
    array = jax.random.normal(rng, extent, jnp.float32) * spread
    if len(cuts) > 0:
        array = level_of(rng, extent, cuts, -0.22, 0.18) * array
    return jnp.clip(array, min=-limit, max=limit).astype(kind)


def setup_inputs(seed: int = 0) -> dict:
    arg_keys = jax.random.split(jax.random.key(seed), 4)
    return {
        "psi": draw_psi(jax.random.fold_in(arg_keys[3], 71), 0),
        "potential": centred(arg_keys[1], (NG, NG, NG), 1.0, 5.0, ((0, 64),), jnp.float32),
        "stick_columns": draw_stick_columns(jax.random.fold_in(arg_keys[3], 71), 0),
    }


def dft_tables(grid_size, freq_count):
    points = jnp.arange(grid_size, dtype=jnp.int32)[:, None]
    freqs = jnp.arange(freq_count, dtype=jnp.int32)[None, :] - freq_count // 2
    phase = (points * freqs) % grid_size
    angle = phase.astype(jnp.float32) * (2.0 * math.pi / grid_size)
    return jnp.cos(angle), jnp.sin(angle)


def complex_product(form, left_re, left_im, right_re, right_im):
    high = lax.Precision.HIGHEST
    real_real = jnp.einsum(form, left_re, right_re, precision=high)
    imag_imag = jnp.einsum(form, left_im, right_im, precision=high)
    real_imag = jnp.einsum(form, left_re, right_im, precision=high)
    imag_real = jnp.einsum(form, left_im, right_re, precision=high)
    return real_real - imag_imag, real_imag + imag_real


def kinetic_factors(columns, freq_count):
    centre = freq_count // 2
    along_u = columns // freq_count - centre
    along_v = columns % freq_count - centre
    along_w = jnp.arange(freq_count, dtype=jnp.int32) - centre
    squared = along_w[:, None] * along_w[:, None] + (along_u * along_u + along_v * along_v)[None, :]
    return 0.5 * squared.astype(jnp.float32) / float(centre * centre)


def margin_of(left, right):
    high = lax.Precision.HIGHEST
    real_part = jnp.einsum("mws,nws->mn", left[0], right[0], precision=high) + jnp.einsum("mws,nws->mn", left[1], right[1], precision=high)
    imag_part = jnp.einsum("mws,nws->mn", left[0], right[1], precision=high) - jnp.einsum("mws,nws->mn", left[1], right[0], precision=high)
    return jnp.stack([real_part, imag_part])


def reference(psi, potential, stick_columns):
    freq_count = psi.shape[2]
    stick_total = psi.shape[3]
    grid_size = potential.shape[0]
    cosine, sine = dft_tables(grid_size, freq_count)

    def apply_band(coeffs):
        column_re, column_im = complex_product("zw,ws->zs", cosine, sine, coeffs[0], coeffs[1])
        flat = jnp.zeros((2, grid_size, freq_count * freq_count), jnp.float32)
        flat = flat.at[:, :, stick_columns].set(jnp.stack([column_re, column_im]))
        freqplane = flat.reshape(2, grid_size, freq_count, freq_count)
        along_y = complex_product("zuv,yv->zuy", freqplane[0], freqplane[1], cosine, sine)
        spatial = complex_product("xu,zuy->zxy", cosine, sine, along_y[0], along_y[1])
        scaled_re = potential * spatial[0]
        scaled_im = potential * spatial[1]
        back_x = complex_product("xu,zxy->zuy", cosine, -sine, scaled_re, scaled_im)
        back_y = complex_product("yv,zuy->zuv", cosine, -sine, back_x[0], back_x[1])
        picked_re = back_y[0].reshape(grid_size, freq_count * freq_count)[:, stick_columns]
        picked_im = back_y[1].reshape(grid_size, freq_count * freq_count)[:, stick_columns]
        applied_re, applied_im = complex_product("zw,zs->ws", cosine, -sine, picked_re, picked_im)
        return jnp.stack([applied_re, applied_im])

    applied = lax.map(apply_band, jnp.moveaxis(psi, 1, 0))
    applied = jnp.moveaxis(applied, 0, 1)
    kinetic = kinetic_factors(stick_columns, freq_count)
    hpsi = kinetic * psi + applied / float(grid_size * grid_size * grid_size)
    margin = margin_of(psi, hpsi) / float(freq_count * stick_total)
    return hpsi, margin
```

```python
import functools
import math

import jax
import jax.numpy as jnp
import numpy as np
from jax import lax
from jax.experimental import pallas as pl
from jax.experimental.pallas import tpu as pltpu
from jax.sharding import PartitionSpec as P

LANES = 128
ROWS = 16


def dft_tables(grid_size, freq_count):
    points = np.arange(grid_size)[:, None]
    freqs = np.arange(freq_count)[None, :] - freq_count // 2
    angle = (points * freqs % grid_size).astype(np.float64) * (2.0 * math.pi / grid_size)
    return np.cos(angle).astype(np.float32), np.sin(angle).astype(np.float32)


def halves(table):
    high = table.astype(jnp.bfloat16)
    low = (table - high.astype(np.float32)).astype(jnp.bfloat16)
    return high, low


def split(value):
    high = value.astype(jnp.bfloat16)
    low = (value - high.astype(jnp.float32)).astype(jnp.bfloat16)
    return high, low


def dot(left, right):
    return jnp.dot(left, right, preferred_element_type=jnp.float32)


def plane_tables(cosine, sine, chunk):
    grid, freqs = cosine.shape
    wide = -(-grid // LANES) * LANES
    wide_v = -(-freqs // LANES) * LANES
    y_out = np.zeros((freqs, 2 * wide), np.float32)
    y_out[:, :grid] = cosine.T
    y_out[:, wide : wide + grid] = sine.T
    y_back = np.zeros((wide, 2 * wide_v), np.float32)
    y_back[:grid, :freqs] = cosine
    y_back[:grid, wide_v : wide_v + freqs] = sine
    x_out = np.stack([cosine.reshape(grid // chunk, chunk, freqs), sine.reshape(grid // chunk, chunk, freqs)], axis=1)
    x_high, x_low = halves(x_out.reshape(2 * grid, freqs))
    x_out = np.concatenate([x_high, x_low, x_high], axis=1)
    b_high, b_low = halves(np.concatenate([cosine.T, sine.T], axis=0))
    x_back = np.concatenate([b_high, b_low, b_high], axis=1)
    return (*halves(y_out), x_out, x_back, *halves(y_back))


def plane_kernel(
    chunk,
    columns,
    recv,
    potential,
    y_out_high,
    y_out_low,
    x_out,
    x_back,
    y_back_high,
    y_back_low,
    send,
    sticks,
    grid_rows,
    flat,
    planes,
    right_x,
    right_b,
):
    planes_held, grid, _ = potential.shape
    freqs = y_out_high.shape[0]
    wide = y_out_high.shape[1] // 2
    wide_v = y_back_high.shape[1] // 2
    blocks = recv.shape[0]
    values = 2 * planes_held
    total = columns.shape[0]
    unroll = 64

    def clear(i, _):
        grid_rows[pl.ds(i * freqs, freqs), :] = jnp.zeros((freqs, LANES), jnp.float32)
        return 0

    lax.fori_loop(0, freqs, clear, 0)
    right_b[...] = jnp.zeros_like(right_b)

    def to_rows(i, _):
        block = jnp.concatenate([recv[i, k] for k in range(recv.shape[1])], axis=0)
        block = jnp.concatenate([block, jnp.zeros((LANES - block.shape[0], LANES), jnp.float32)], axis=0)
        turned = block.T
        sticks[pl.ds(i * 2 * LANES, LANES), :] = turned
        sticks[pl.ds(i * 2 * LANES + LANES, LANES), :] = pltpu.roll(turned, LANES - values, 1)
        return 0

    lax.fori_loop(0, blocks, to_rows, 0)

    def scatter(i, _):
        base = i * unroll
        rows = [sticks[pl.ds(base + j, 1), :] for j in range(unroll)]
        for j in range(unroll):
            grid_rows[pl.ds(columns[base + j], 1), :] = rows[j]
        return 0

    lax.fori_loop(0, total // unroll, scatter, 0)

    def to_planes(u, _):
        turned = grid_rows[pl.ds(u * freqs, freqs), :].T
        for k in range(flat.shape[0]):
            upper = min(freqs - k * LANES, LANES)
            flat[k, pl.ds(u * ROWS, ROWS), 0:upper] = turned[0:ROWS, k * LANES : k * LANES + upper]
        return 0

    lax.fori_loop(0, freqs, to_planes, 0)

    def plane(z, _):
        real, imag = (
            jnp.concatenate([flat[k, pl.ds(at, freqs, stride=ROWS), :] for k in range(flat.shape[0])], axis=1)[:, :freqs]
            for at in (z, planes_held + z)
        )
        high, low = split(jnp.concatenate([real, imag], axis=0))
        prod = dot(high, y_out_high[...]) + dot(low, y_out_high[...]) + dot(high, y_out_low[...])
        along_re = prod[:freqs, :wide] - prod[freqs:, wide:]
        along_im = prod[:freqs, wide:] + prod[freqs:, :wide]
        high, low = split(jnp.concatenate([along_re, along_im], axis=1))
        right_x[0:freqs, :] = high
        right_x[freqs : 2 * freqs, :] = high
        right_x[2 * freqs : 3 * freqs, :] = low

        def part(i, _):
            prod = dot(x_out[pl.ds(i * 2 * chunk, 2 * chunk), :], right_x[...])
            here = potential[z, pl.ds(i * chunk, chunk), :]
            real = (prod[:chunk, :wide] - prod[chunk:, wide:])[:, :grid] * here
            imag = (prod[:chunk, wide:] + prod[chunk:, :wide])[:, :grid] * here
            for value, at in ((real, 0), (imag, wide)):
                high, low = split(value)
                right_b[pl.ds(i * chunk, chunk), at : at + grid] = high
                right_b[pl.ds(grid + i * chunk, chunk), at : at + grid] = high
                right_b[pl.ds(2 * grid + i * chunk, chunk), at : at + grid] = low
            return 0

        lax.fori_loop(0, grid // chunk, part, 0)
        prod = dot(x_back[...], right_b[...])
        back_re = prod[:freqs, :wide] + prod[freqs:, wide:]
        back_im = prod[:freqs, wide:] - prod[freqs:, :wide]
        high, low = split(jnp.concatenate([back_re, back_im], axis=0))
        prod = dot(high, y_back_high[...]) + dot(low, y_back_high[...]) + dot(high, y_back_low[...])
        done_re = prod[:freqs, :wide_v] + prod[freqs:, wide_v:]
        done_im = prod[freqs:, :wide_v] - prod[:freqs, wide_v:]
        for k in range(planes.shape[0]):
            planes[k, pl.ds(z * freqs, freqs), :] = done_re[:, k * LANES : (k + 1) * LANES]
            planes[k, pl.ds((planes_held + z) * freqs, freqs), :] = done_im[:, k * LANES : (k + 1) * LANES]
        return 0

    lax.fori_loop(0, planes_held, plane, 0)

    def from_planes(u, _):
        for k in range(planes.shape[0]):
            upper = min(freqs - k * LANES, LANES)
            turned = planes[k, pl.ds(u, ROWS, stride=freqs), :].T
            grid_rows[pl.ds(u * freqs + k * LANES, upper), 0:ROWS] = turned[:upper]
        return 0

    lax.fori_loop(0, freqs, from_planes, 0)

    def gather(i, _):
        base = i * unroll
        rows = [grid_rows[pl.ds(columns[base + j], 1), :] for j in range(unroll)]
        for j in range(unroll):
            sticks[pl.ds(base + j, 1), :] = rows[j]
        return 0

    lax.fori_loop(0, total // unroll, gather, 0)

    def from_rows(i, _):
        first = sticks[pl.ds(i * 2 * LANES, LANES), :].T[:values]
        second = sticks[pl.ds(i * 2 * LANES + LANES, LANES), :].T[:values]
        block = jnp.concatenate([first, second], axis=0)
        depth = send.shape[2]
        for k in range(send.shape[1]):
            send[i, k] = block[k * depth : (k + 1) * depth]
        return 0

    lax.fori_loop(0, blocks, from_rows, 0)


def plane_call(recv, potential, columns, cosine, sine):
    planes_held, grid, _ = potential.shape
    freqs = cosine.shape[1]
    chunk = 64
    tables = plane_tables(cosine, sine, chunk)
    wide = tables[0].shape[1] // 2
    wide_v = tables[4].shape[1] // 2
    vmem = pl.BlockSpec(memory_space=pltpu.VMEM)
    return pl.pallas_call(
        functools.partial(plane_kernel, chunk),
        out_shape=jax.ShapeDtypeStruct(recv.shape, jnp.float32),
        in_specs=[pl.BlockSpec(memory_space=pltpu.SMEM)] + [vmem] * 8,
        out_specs=vmem,
        scratch_shapes=[
            pltpu.VMEM((columns.shape[0], LANES), jnp.float32),
            pltpu.VMEM((freqs * freqs, LANES), jnp.float32),
            pltpu.VMEM((wide_v // LANES, freqs * ROWS, LANES), jnp.float32),
            pltpu.VMEM((wide_v // LANES, ROWS * freqs, LANES), jnp.float32),
            pltpu.VMEM((3 * freqs, 2 * wide), jnp.bfloat16),
            pltpu.VMEM((3 * grid, 2 * wide), jnp.bfloat16),
        ],
        compiler_params=pltpu.CompilerParams(vmem_limit_bytes=56 * 1024 * 1024),
        name="planes",
    )(columns, recv, potential, *tables)


def kinetic_factors(columns, freq_count):
    centre = freq_count // 2
    along_u = columns // freq_count - centre
    along_v = columns % freq_count - centre
    along_w = jnp.arange(freq_count, dtype=jnp.int32) - centre
    squared = along_w[:, None] * along_w[:, None] + (along_u * along_u + along_v * along_v)[None, :]
    return 0.5 * squared.astype(jnp.float32) / float(centre * centre)


def margin_of(left, right):
    high = lax.Precision.HIGHEST
    real_part = jnp.einsum("mws,nws->mn", left[0], right[0], precision=high) + jnp.einsum(
        "mws,nws->mn", left[1], right[1], precision=high
    )
    imag_part = jnp.einsum("mws,nws->mn", left[0], right[1], precision=high) - jnp.einsum(
        "mws,nws->mn", left[1], right[0], precision=high
    )
    return jnp.stack([real_part, imag_part])


def on_device(psi, potential, stick_columns):
    freq_count = psi.shape[2]
    per_device = psi.shape[3]
    grid_size = potential.shape[1]
    plane_count = potential.shape[0]
    fft_count = lax.axis_size("fft")
    position = lax.axis_index("fft")
    cosine, sine = dft_tables(grid_size, freq_count)
    table = np.stack([np.stack([cosine, -sine], 1), np.stack([sine, cosine], 1)])
    table = table.reshape(2, fft_count, plane_count, 2 * freq_count).transpose(1, 0, 2, 3)
    table = table.reshape(fft_count * 2 * plane_count, 2 * freq_count)
    my_columns = lax.dynamic_slice_in_dim(stick_columns, position * per_device, per_device)
    sent = jnp.dot(table, psi.reshape(2 * freq_count, per_device), precision=lax.Precision.HIGH)
    halves_of = per_device // LANES
    sent = sent.reshape(fft_count, 2 * plane_count, halves_of, LANES).transpose(0, 2, 1, 3)
    sent = sent.reshape(fft_count, plane_count, 4, LANES)
    moved = lax.all_to_all(sent, "fft", split_axis=0, concat_axis=0, tiled=True)
    picked = plane_call(moved, potential, stick_columns, cosine, sine)
    returned = lax.all_to_all(picked, "fft", split_axis=0, concat_axis=0, tiled=True)
    returned = returned.reshape(fft_count, halves_of, 2 * plane_count, LANES).transpose(0, 2, 1, 3)
    returned = returned.reshape(fft_count * 2 * plane_count, per_device)
    applied = jnp.dot(table.T, returned, precision=lax.Precision.HIGH).reshape(psi.shape)
    kinetic = kinetic_factors(my_columns, freq_count)
    hpsi = kinetic * psi + applied / float(grid_size * grid_size * grid_size)
    partial_sums = margin_of(lax.all_gather(psi, "band", axis=1, tiled=True), hpsi)
    totals = lax.psum(partial_sums, "fft")
    margin = totals / float(freq_count * per_device * fft_count)
    return (hpsi, margin)


def solution(mesh):
    placed = (P(None, "band", None, "fft"), P("fft", None, None), P())
    return jax.shard_map(
        on_device,
        mesh=mesh,
        in_specs=placed,
        out_specs=(P(None, "band", None, "fft"), P(None, None, "band")),
        check_vma=False,
    )
```

```python
import functools
import math

import jax
import jax.numpy as jnp
import numpy as np
from jax import lax
from jax.experimental import pallas as pl
from jax.experimental.pallas import tpu as pltpu
from jax.sharding import PartitionSpec as P

LANES = 128
ROWS = 16
MESH = pl.DeviceIdType.MESH


def dft_tables(grid_size, freq_count):
    points = np.arange(grid_size)[:, None]
    freqs = np.arange(freq_count)[None, :] - freq_count // 2
    angle = (points * freqs % grid_size).astype(np.float64) * (2.0 * math.pi / grid_size)
    return np.cos(angle).astype(np.float32), np.sin(angle).astype(np.float32)


def halves(table):
    high = table.astype(jnp.bfloat16)
    low = (table - high.astype(np.float32)).astype(jnp.bfloat16)
    return high, low


def split(value):
    high = value.astype(jnp.bfloat16)
    low = (value - high.astype(jnp.float32)).astype(jnp.bfloat16)
    return high, low


def dot(left, right):
    return jnp.dot(left, right, preferred_element_type=jnp.float32)


def plane_tables(cosine, sine, chunk):
    grid, freqs = cosine.shape
    wide = -(-grid // LANES) * LANES
    wide_v = -(-freqs // LANES) * LANES
    y_out = np.zeros((freqs, 2 * wide), np.float32)
    y_out[:, :grid] = cosine.T
    y_out[:, wide : wide + grid] = sine.T
    y_back = np.zeros((wide, 2 * wide_v), np.float32)
    y_back[:grid, :freqs] = cosine
    y_back[:grid, wide_v : wide_v + freqs] = sine
    x_out = np.stack([cosine.reshape(grid // chunk, chunk, freqs), sine.reshape(grid // chunk, chunk, freqs)], axis=1)
    x_high, x_low = halves(x_out.reshape(2 * grid, freqs))
    x_out = np.concatenate([x_high, x_low, x_high], axis=1)
    b_high, b_low = halves(np.concatenate([cosine.T, sine.T], axis=0))
    x_back = np.concatenate([b_high, b_low, b_high], axis=1)
    return (*halves(y_out), x_out, x_back, *halves(y_back))


def plane_kernel(
    chunk,
    columns,
    recv,
    potential,
    y_out_high,
    y_out_low,
    x_out,
    x_back,
    y_back_high,
    y_back_low,
    send,
    sticks,
    grid_rows,
    flat,
    planes,
    right_x,
    right_b,
):
    planes_held, grid, _ = potential.shape
    freqs = y_out_high.shape[0]
    wide = y_out_high.shape[1] // 2
    wide_v = y_back_high.shape[1] // 2
    blocks = recv.shape[0]
    values = 2 * planes_held
    total = columns.shape[0]
    unroll = 64

    def clear(i, _):
        grid_rows[pl.ds(i * freqs, freqs), :] = jnp.zeros((freqs, LANES), jnp.float32)
        return 0

    lax.fori_loop(0, freqs, clear, 0)
    right_b[...] = jnp.zeros_like(right_b)

    def to_rows(i, _):
        block = jnp.concatenate([recv[i, k] for k in range(recv.shape[1])], axis=0)
        block = jnp.concatenate([block, jnp.zeros((LANES - block.shape[0], LANES), jnp.float32)], axis=0)
        turned = block.T
        sticks[pl.ds(i * 2 * LANES, LANES), :] = turned
        sticks[pl.ds(i * 2 * LANES + LANES, LANES), :] = pltpu.roll(turned, LANES - values, 1)
        return 0

    lax.fori_loop(0, blocks, to_rows, 0, unroll=4)

    def scatter(i, _):
        base = i * unroll
        rows = [sticks[pl.ds(base + j, 1), :] for j in range(unroll)]
        for j in range(unroll):
            grid_rows[pl.ds(columns[base + j], 1), :] = rows[j]
        return 0

    lax.fori_loop(0, total // unroll, scatter, 0)

    def to_planes(u, _):
        turned = grid_rows[pl.ds(u * freqs, freqs), :].T
        for k in range(flat.shape[0]):
            upper = min(freqs - k * LANES, LANES)
            flat[k, pl.ds(u * ROWS, ROWS), 0:upper] = turned[0:ROWS, k * LANES : k * LANES + upper]
        return 0

    lax.fori_loop(0, freqs, to_planes, 0, unroll=8)

    def plane(z, _):
        real, imag = (
            jnp.concatenate([flat[k, pl.ds(at, freqs, stride=ROWS), :] for k in range(flat.shape[0])], axis=1)[:, :freqs]
            for at in (z, planes_held + z)
        )
        high, low = split(jnp.concatenate([real, imag], axis=0))
        prod = dot(high, y_out_high[...]) + dot(low, y_out_high[...]) + dot(high, y_out_low[...])
        along_re = prod[:freqs, :wide] - prod[freqs:, wide:]
        along_im = prod[:freqs, wide:] + prod[freqs:, :wide]
        high, low = split(jnp.concatenate([along_re, along_im], axis=1))
        right_x[0:freqs, :] = high
        right_x[freqs : 2 * freqs, :] = high
        right_x[2 * freqs : 3 * freqs, :] = low

        def part(i, _):
            prod = dot(x_out[pl.ds(i * 2 * chunk, 2 * chunk), :], right_x[...])
            here = potential[z, pl.ds(i * chunk, chunk), :]
            real = (prod[:chunk, :wide] - prod[chunk:, wide:])[:, :grid] * here
            imag = (prod[:chunk, wide:] + prod[chunk:, :wide])[:, :grid] * here
            for value, at in ((real, 0), (imag, wide)):
                high, low = split(value)
                right_b[pl.ds(i * chunk, chunk), at : at + grid] = high
                right_b[pl.ds(grid + i * chunk, chunk), at : at + grid] = high
                right_b[pl.ds(2 * grid + i * chunk, chunk), at : at + grid] = low
            return 0

        lax.fori_loop(0, grid // chunk, part, 0)
        prod = dot(x_back[...], right_b[...])
        back_re = prod[:freqs, :wide] + prod[freqs:, wide:]
        back_im = prod[:freqs, wide:] - prod[freqs:, :wide]
        high, low = split(jnp.concatenate([back_re, back_im], axis=0))
        prod = dot(high, y_back_high[...]) + dot(low, y_back_high[...]) + dot(high, y_back_low[...])
        done_re = prod[:freqs, :wide_v] + prod[freqs:, wide_v:]
        done_im = prod[freqs:, :wide_v] - prod[:freqs, wide_v:]
        for k in range(planes.shape[0]):
            planes[k, pl.ds(z * freqs, freqs), :] = done_re[:, k * LANES : (k + 1) * LANES]
            planes[k, pl.ds((planes_held + z) * freqs, freqs), :] = done_im[:, k * LANES : (k + 1) * LANES]
        return 0

    lax.fori_loop(0, planes_held, plane, 0)

    def from_planes(u, _):
        for k in range(planes.shape[0]):
            upper = min(freqs - k * LANES, LANES)
            turned = planes[k, pl.ds(u, ROWS, stride=freqs), :].T
            grid_rows[pl.ds(u * freqs + k * LANES, upper), 0:ROWS] = turned[:upper]
        return 0

    lax.fori_loop(0, freqs, from_planes, 0, unroll=8)

    def gather(i, _):
        base = i * unroll
        rows = [grid_rows[pl.ds(columns[base + j], 1), :] for j in range(unroll)]
        for j in range(unroll):
            sticks[pl.ds(base + j, 1), :] = rows[j]
        return 0

    lax.fori_loop(0, total // unroll, gather, 0)

    def from_rows(i, _):
        first = sticks[pl.ds(i * 2 * LANES, LANES), :].T[:values]
        second = sticks[pl.ds(i * 2 * LANES + LANES, LANES), :].T[:values]
        block = jnp.concatenate([first, second], axis=0)
        depth = send.shape[2]
        for k in range(send.shape[1]):
            send[i, k] = block[k * depth : (k + 1) * depth]
        return 0

    lax.fori_loop(0, blocks, from_rows, 0, unroll=4)


def plane_call(recv, potential, columns, cosine, sine):
    planes_held, grid, _ = potential.shape
    freqs = cosine.shape[1]
    chunk = 64
    tables = plane_tables(cosine, sine, chunk)
    wide = tables[0].shape[1] // 2
    wide_v = tables[4].shape[1] // 2
    vmem = pl.BlockSpec(memory_space=pltpu.VMEM)
    return pl.pallas_call(
        functools.partial(plane_kernel, chunk),
        out_shape=jax.ShapeDtypeStruct(recv.shape, jnp.float32),
        in_specs=[pl.BlockSpec(memory_space=pltpu.SMEM)] + [vmem] * 8,
        out_specs=vmem,
        scratch_shapes=[
            pltpu.VMEM((columns.shape[0], LANES), jnp.float32),
            pltpu.VMEM((freqs * freqs, LANES), jnp.float32),
            pltpu.VMEM((wide_v // LANES, freqs * ROWS, LANES), jnp.float32),
            pltpu.VMEM((wide_v // LANES, ROWS * freqs, LANES), jnp.float32),
            pltpu.VMEM((3 * freqs, 2 * wide), jnp.bfloat16),
            pltpu.VMEM((3 * grid, 2 * wide), jnp.bfloat16),
        ],
        compiler_params=pltpu.CompilerParams(vmem_limit_bytes=56 * 1024 * 1024),
        name="planes",
    )(columns, recv, potential, *tables)


def kinetic_factors(columns, freq_count):
    centre = freq_count // 2
    along_u = columns // freq_count - centre
    along_v = columns % freq_count - centre
    along_w = jnp.arange(freq_count, dtype=jnp.int32) - centre
    squared = along_w[:, None] * along_w[:, None] + (along_u * along_u + along_v * along_v)[None, :]
    return 0.5 * squared.astype(jnp.float32) / float(centre * centre)


def greet(position, count):
    barrier = pltpu.get_barrier_semaphore()

    def signal(k, _):
        pl.semaphore_signal(barrier, inc=1, device_id={"fft": lax.rem(position + k, count)}, device_id_type=MESH)
        return 0

    lax.fori_loop(1, count, signal, 0)
    return barrier


def await_others(buffer, semaphore):
    others = buffer.at[pl.ds(0, buffer.shape[0] - 1)]
    pltpu.make_async_copy(others, others, semaphore).wait()


def spread_kernel(psi, table_high, table_low, recv, staged, send, send_sem, recv_sem):
    count, pieces, depth, _ = recv.shape
    values = pieces * depth // 2
    position = lax.axis_index("fft")
    barrier = greet(position, count)
    high, low = split(psi[...])
    staged[...] = dot(table_high[...], high) + dot(table_low[...], high) + dot(table_high[...], low)
    pl.semaphore_wait(barrier, count - 1)

    def stage(peer):
        rows = staged[pl.ds(peer * ROWS, ROWS), :]
        block = jnp.concatenate([rows[:values, :LANES], rows[:values, LANES:]], axis=0)
        return [block[k * depth : (k + 1) * depth] for k in range(pieces)]

    def post(k, _):
        peer = lax.rem(position + k, count)
        for at, piece in enumerate(stage(peer)):
            send[peer, at] = piece
        pltpu.make_async_remote_copy(
            src_ref=send.at[peer],
            dst_ref=recv.at[position],
            send_sem=send_sem,
            recv_sem=recv_sem,
            device_id={"fft": peer},
            device_id_type=MESH,
        ).start()
        return 0

    lax.fori_loop(1, count, post, 0)
    for at, piece in enumerate(stage(position)):
        recv[position, at] = piece
    await_others(recv, recv_sem)
    await_others(recv, send_sem)


def spread_call(psi, table, count, planes_held):
    rows = table.shape[0]
    vmem = pl.BlockSpec(memory_space=pltpu.VMEM)
    shape = (count, planes_held, 2 * psi.shape[1] // LANES, LANES)
    return pl.pallas_call(
        spread_kernel,
        out_shape=jax.ShapeDtypeStruct(shape, jnp.float32),
        in_specs=[vmem] * 3,
        out_specs=vmem,
        scratch_shapes=[
            pltpu.VMEM((rows, psi.shape[1]), jnp.float32),
            pltpu.VMEM(shape, jnp.float32),
            pltpu.SemaphoreType.DMA,
            pltpu.SemaphoreType.DMA,
        ],
        compiler_params=pltpu.CompilerParams(
            collective_id=0, has_side_effects=True, vmem_limit_bytes=32 * 1024 * 1024
        ),
        name="spread",
    )(psi, *halves(table))


def collect_kernel(
    scale,
    weight,
    picked,
    psi,
    bands,
    kinetic,
    table_high,
    table_low,
    hpsi,
    margin,
    got,
    right,
    sums,
    send_sem,
    recv_sem,
    sum_send_sem,
    sum_recv_sem,
):
    count, pieces, depth, _ = picked.shape
    values = pieces * depth // 2
    freqs = kinetic.shape[0]
    position = lax.axis_index("fft")
    barrier = greet(position, count)
    pl.semaphore_wait(barrier, count - 1)

    def post(k, _):
        peer = lax.rem(position + k, count)
        pltpu.make_async_remote_copy(
            src_ref=picked.at[peer],
            dst_ref=got.at[position],
            send_sem=send_sem,
            recv_sem=recv_sem,
            device_id={"fft": peer},
            device_id_type=MESH,
        ).start()
        return 0

    lax.fori_loop(1, count, post, 0)
    got[position] = picked[position]
    await_others(got, recv_sem)

    def to_right(i, _):
        block = jnp.concatenate([got[i, k] for k in range(pieces)], axis=0)
        blank = jnp.zeros((ROWS - values, LANES), jnp.float32)
        at = pl.multiple_of(i * ROWS, ROWS)
        right[pl.ds(at, ROWS), 0:LANES] = jnp.concatenate([block[:values], blank], axis=0)
        right[pl.ds(at, ROWS), LANES : 2 * LANES] = jnp.concatenate([block[values:], blank], axis=0)
        return 0

    lax.fori_loop(0, count, to_right, 0, unroll=4)
    high, low = split(right[...])
    applied = dot(table_high[...], high) + dot(table_low[...], high) + dot(table_high[...], low)
    hpsi[0:freqs, :] = kinetic[...] * psi[0:freqs, :] + applied[:freqs] * scale
    hpsi[freqs : 2 * freqs, :] = kinetic[...] * psi[freqs : 2 * freqs, :] + applied[freqs:] * scale

    def folded(product):
        narrow = product[:, :LANES] + product[:, LANES:]
        return jnp.sum(narrow, axis=0, keepdims=True)

    real_rows, imag_rows = [], []
    for m in range(bands.shape[0]):
        left_re, left_im = bands[m, 0:freqs, :], bands[m, freqs : 2 * freqs, :]
        right_re, right_im = hpsi[0:freqs, :], hpsi[freqs : 2 * freqs, :]
        real_rows.append(folded(left_re * right_re + left_im * right_im))
        imag_rows.append(folded(left_re * right_im - left_im * right_re))
    sums[position] = jnp.concatenate(real_rows + imag_rows, axis=0) * weight

    def post_sums(k, _):
        pltpu.make_async_remote_copy(
            src_ref=sums.at[position],
            dst_ref=sums.at[position],
            send_sem=sum_send_sem,
            recv_sem=sum_recv_sem,
            device_id={"fft": lax.rem(position + k, count)},
            device_id_type=MESH,
        ).start()
        return 0

    lax.fori_loop(1, count, post_sums, 0)
    await_others(sums, sum_recv_sem)
    margin[...] = jnp.sum(jnp.sum(sums[...], axis=0), axis=1, keepdims=True)
    await_others(got, send_sem)
    await_others(sums, sum_send_sem)


def collect_call(picked, psi, bands, kinetic, table, scale, weight):
    count = picked.shape[0]
    vmem = pl.BlockSpec(memory_space=pltpu.VMEM)
    height = 2 * bands.shape[0]
    return pl.pallas_call(
        functools.partial(collect_kernel, scale, weight),
        out_shape=(jax.ShapeDtypeStruct(psi.shape, jnp.float32), jax.ShapeDtypeStruct((height, 1), jnp.float32)),
        in_specs=[vmem] * 6,
        out_specs=(vmem, vmem),
        scratch_shapes=[
            pltpu.VMEM(picked.shape, jnp.float32),
            pltpu.VMEM((count * ROWS, psi.shape[1]), jnp.float32),
            pltpu.VMEM((count, height, LANES), jnp.float32),
            pltpu.SemaphoreType.DMA,
            pltpu.SemaphoreType.DMA,
            pltpu.SemaphoreType.DMA,
            pltpu.SemaphoreType.DMA,
        ],
        compiler_params=pltpu.CompilerParams(
            collective_id=1, has_side_effects=True, vmem_limit_bytes=32 * 1024 * 1024
        ),
        name="collect",
    )(picked, psi, bands, kinetic, *halves(table.T))


def on_device(psi, potential, stick_columns):
    freq_count = psi.shape[2]
    per_device = psi.shape[3]
    grid_size = potential.shape[1]
    plane_count = potential.shape[0]
    fft_count = lax.axis_size("fft")
    position = lax.axis_index("fft")
    cosine, sine = dft_tables(grid_size, freq_count)
    table = np.stack([np.concatenate([cosine, -sine], 1), np.concatenate([sine, cosine], 1)])
    table = table.reshape(2, fft_count, plane_count, 2 * freq_count).transpose(1, 0, 2, 3)
    table = table.reshape(fft_count, 2 * plane_count, 2 * freq_count)
    table = np.pad(table, ((0, 0), (0, ROWS - 2 * plane_count), (0, 0))).reshape(fft_count * ROWS, 2 * freq_count)
    flat_psi = psi.reshape(2 * freq_count, per_device)
    moved = spread_call(flat_psi, table, fft_count, plane_count)
    picked = plane_call(moved, potential, stick_columns, cosine, sine)
    bands = lax.all_gather(flat_psi, "band", axis=0)
    my_columns = lax.dynamic_slice_in_dim(stick_columns, position * per_device, per_device)
    kinetic = kinetic_factors(my_columns, freq_count)
    scale = 1.0 / float(grid_size * grid_size * grid_size)
    weight = 1.0 / float(freq_count * per_device * fft_count)
    hpsi, margin = collect_call(picked, flat_psi, bands, kinetic, table, scale, weight)
    return (hpsi.reshape(psi.shape), margin.reshape(2, bands.shape[0], 1))


def solution(mesh):
    placed = (P(None, "band", None, "fft"), P("fft", None, None), P())
    return jax.shard_map(
        on_device,
        mesh=mesh,
        in_specs=placed,
        out_specs=(P(None, "band", None, "fft"), P(None, None, "band")),
        check_vma=False,
    )
```

```python
import functools
import math

import jax
import jax.numpy as jnp
import numpy as np
from jax import lax
from jax.experimental import pallas as pl
from jax.experimental.pallas import tpu as pltpu
from jax.sharding import PartitionSpec as P

LANES = 128
ROWS = 16
MESH = pl.DeviceIdType.MESH


def dft_tables(grid_size, freq_count):
    points = np.arange(grid_size)[:, None]
    freqs = np.arange(freq_count)[None, :] - freq_count // 2
    angle = (points * freqs % grid_size).astype(np.float64) * (2.0 * math.pi / grid_size)
    return np.cos(angle).astype(np.float32), np.sin(angle).astype(np.float32)


def halves(table):
    high = table.astype(jnp.bfloat16)
    low = (table - high.astype(np.float32)).astype(jnp.bfloat16)
    return high, low


def split(value):
    high = value.astype(jnp.bfloat16)
    low = (value - high.astype(jnp.float32)).astype(jnp.bfloat16)
    return high, low


def dot(left, right):
    return jnp.dot(left, right, preferred_element_type=jnp.float32)


def packed_rows(table, whole):
    high, low = halves(table)
    tail = table.shape[0] - whole
    spare = np.zeros((-3 * tail % LANES, table.shape[1]), high.dtype)
    if whole % (2 * LANES) == 0:
        spare = np.zeros((-3 * tail % (2 * LANES), table.shape[1]), high.dtype)
    return np.concatenate([high[:whole], high[:whole], low[:whole], high[whole:], high[whole:], low[whole:], spare], axis=0)


def packed_columns(value, whole, tail):
    high, low = split(value)
    rest_high = high[:, whole : whole + LANES].astype(jnp.float32)
    rest_low = low[:, whole : whole + LANES].astype(jnp.float32)
    parts = [high[:, :whole], low[:, :whole], high[:, :whole]]
    if 3 * tail <= LANES:
        rest = rest_high + pltpu.roll(rest_low, tail, 1) + pltpu.roll(rest_high, 2 * tail, 1)
        parts.append(rest.astype(jnp.bfloat16))
    else:
        parts.append((rest_high + pltpu.roll(rest_low, tail, 1)).astype(jnp.bfloat16))
        parts.append(rest_high.astype(jnp.bfloat16))
    return jnp.concatenate(parts, axis=1)


def three(table):
    high, low = halves(table)
    return np.concatenate([high, low, high], axis=1)


def whole_lanes(count):
    return count // LANES * LANES


def plane_tables(cosine, sine):
    grid, freqs = cosine.shape
    half = grid // 2
    wide = -(-grid // LANES) * LANES
    wide_v = -(-freqs // LANES) * LANES
    y_out = np.zeros((freqs, 2 * wide), np.float32)
    y_out[:, :grid] = cosine.T
    y_out[:, wide : wide + grid] = sine.T
    y_back = np.zeros((grid, 2 * wide_v), np.float32)
    y_back[:, :freqs] = cosine
    y_back[:, wide_v : wide_v + freqs] = sine
    x_out = [three(np.concatenate([cosine[:half, k::2], sine[:half, k::2]], axis=0)) for k in (0, 1)]
    x_back = [three(np.concatenate([cosine[:half, k::2].T, sine[:half, k::2].T], axis=0)) for k in (0, 1)]
    return (
        packed_rows(y_out, whole_lanes(freqs)),
        np.stack(x_out),
        np.stack(x_back),
        packed_rows(y_back, whole_lanes(grid)),
    )


def stacked(value):
    high, low = split(value)
    return jnp.concatenate([high, high, low], axis=0)


def complex_parts(prod, rows, wide, sign):
    real = prod[:rows, :wide] - sign * prod[rows:, wide:]
    imag = prod[:rows, wide:] + sign * prod[rows:, :wide]
    return real, imag


def walk(columns, index, index_sem, visit):
    chunk = index.shape[0] // 2
    pairs = columns.shape[0] // (2 * chunk)

    def fetch(number, slot):
        source = columns.at[pl.ds(pl.multiple_of(number * chunk, chunk), chunk)]
        return pltpu.make_async_copy(source, index.at[pl.ds(slot * chunk, chunk)], index_sem.at[slot])

    fetch(0, 0).start()

    def pair(i, _):
        fetch(2 * i + 1, 1).start()
        fetch(2 * i, 0).wait()
        visit(2 * i * chunk, 0, chunk)

        @pl.when(i < pairs - 1)
        def _():
            fetch(2 * i + 2, 0).start()

        fetch(2 * i + 1, 1).wait()
        visit(2 * i * chunk + chunk, chunk, chunk)
        return 0

    lax.fori_loop(0, pairs, pair, 0)


def plane_kernel(
    columns,
    recv,
    potential_hbm,
    y_out_hbm,
    x_out_hbm,
    x_back_hbm,
    y_back_hbm,
    send,
    sticks,
    grid_rows,
    flat,
    planes,
    potential,
    y_out,
    x_out,
    x_back,
    y_back,
    index,
    load_sem,
    index_sem,
):
    planes_held, grid, _ = potential.shape
    half = grid // 2
    freqs = x_back.shape[1]
    even = freqs // 2
    wide = y_out.shape[1] // 2
    wide_v = y_back.shape[1] // 2
    blocks = recv.shape[0]
    values = 2 * planes_held
    batch = 64

    loads = start_loads(
        (
            (potential_hbm, potential),
            (y_out_hbm, y_out),
            (x_out_hbm, x_out),
            (x_back_hbm, x_back),
            (y_back_hbm, y_back),
        ),
        load_sem,
    )

    def clear(i, _):
        grid_rows[pl.ds(i * freqs, freqs), :] = jnp.zeros((freqs, LANES), jnp.float32)
        return 0

    lax.fori_loop(0, freqs, clear, 0)

    def to_rows(i, _):
        block = jnp.concatenate([recv[i, k] for k in range(recv.shape[1])], axis=0)
        block = jnp.concatenate([block, jnp.zeros((LANES - block.shape[0], LANES), jnp.float32)], axis=0)
        turned = block.T
        sticks[pl.ds(i * 2 * LANES, LANES), :] = turned
        sticks[pl.ds(i * 2 * LANES + LANES, LANES), :] = pltpu.roll(turned, LANES - values, 1)
        return 0

    lax.fori_loop(0, blocks, to_rows, 0, unroll=4)

    def scatter(base, offset, count):
        base = pl.multiple_of(base, count)
        for k in range(0, count, batch):
            rows = [sticks[pl.ds(base + k + j, 1), :] for j in range(batch)]
            for j in range(batch):
                grid_rows[pl.ds(index[offset + k + j], 1), :] = rows[j]

    walk(columns, index, index_sem, scatter)

    def to_planes(u, _):
        turned = grid_rows[pl.ds(u * freqs, freqs), :].T
        for k in range(flat.shape[0]):
            upper = min(freqs - k * LANES, LANES)
            flat[k, pl.ds(u * ROWS, ROWS), 0:upper] = turned[0:ROWS, k * LANES : k * LANES + upper]
        return 0

    lax.fori_loop(0, freqs, to_planes, 0, unroll=8)
    for load in loads:
        load.wait()

    def plane(z, _):
        lane = lax.broadcasted_iota(jnp.int32, (2 * freqs, LANES), 1)
        tiles = []
        for k in range(flat.shape[0]):
            pair = [flat[k, pl.ds(at, freqs, stride=ROWS), :] for at in (z, planes_held + z)]
            pair = jnp.concatenate(pair, axis=0)
            tiles.append(pair if freqs - k * LANES >= LANES else jnp.where(lane < freqs - k * LANES, pair, 0.0))
        left = packed_columns(jnp.concatenate(tiles, axis=1), whole_lanes(freqs), freqs % LANES)
        along = jnp.concatenate(complex_parts(dot(left, y_out[...]), freqs, wide, 1.0), axis=1)
        first_re, first_im = complex_parts(dot(x_out[0], stacked(along[:even])), half, wide, 1.0)
        second_re, second_im = complex_parts(dot(x_out[1], stacked(along[even:])), half, wide, 1.0)
        lower = potential[z, 0:half, :]
        upper = potential[z, half:grid, :]
        blank = jnp.zeros((half, wide - grid), jnp.float32)
        lower = jnp.concatenate([lower, blank], axis=1)
        upper = jnp.concatenate([upper, blank], axis=1)
        low_re, low_im = (first_re + second_re) * lower, (first_im + second_im) * lower
        up_re, up_im = (first_re - second_re) * upper, (first_im - second_im) * upper
        added = jnp.concatenate([low_re + up_re, low_im + up_im], axis=1)
        taken = jnp.concatenate([low_re - up_re, low_im - up_im], axis=1)
        even_re, even_im = complex_parts(dot(x_back[0], stacked(added)), even, wide, -1.0)
        odd_re, odd_im = complex_parts(dot(x_back[1], stacked(taken)), even, wide, -1.0)
        left = packed_columns(
            jnp.concatenate([even_re, odd_re, even_im, odd_im], axis=0), whole_lanes(grid), grid % LANES
        )
        prod = dot(left, y_back[...])
        done_re = prod[:freqs, :wide_v] + prod[freqs:, wide_v:]
        done_im = prod[freqs:, :wide_v] - prod[:freqs, wide_v:]
        for k in range(planes.shape[0]):
            planes[k, pl.ds(z * freqs, freqs), :] = done_re[:, k * LANES : (k + 1) * LANES]
            planes[k, pl.ds((planes_held + z) * freqs, freqs), :] = done_im[:, k * LANES : (k + 1) * LANES]
        return 0

    lax.fori_loop(0, planes_held, plane, 0)

    def from_planes(u, _):
        for k in range(planes.shape[0]):
            upper = min(freqs - k * LANES, LANES)
            turned = planes[k, pl.ds(u, ROWS, stride=freqs), :].T
            grid_rows[pl.ds(u * freqs + k * LANES, upper), 0:ROWS] = turned[:upper]
        return 0

    lax.fori_loop(0, freqs, from_planes, 0, unroll=8)

    def gather(base, offset, count):
        base = pl.multiple_of(base, count)
        for k in range(0, count, batch):
            rows = [grid_rows[pl.ds(index[offset + k + j], 1), :] for j in range(batch)]
            for j in range(batch):
                sticks[pl.ds(base + k + j, 1), :] = rows[j]

    walk(columns, index, index_sem, gather)

    def from_rows(i, _):
        first = sticks[pl.ds(i * 2 * LANES, LANES), :].T[:values]
        second = sticks[pl.ds(i * 2 * LANES + LANES, LANES), :].T[:values]
        block = jnp.concatenate([first, second], axis=0)
        depth = send.shape[2]
        for k in range(send.shape[1]):
            send[i, k] = block[k * depth : (k + 1) * depth]
        return 0

    lax.fori_loop(0, blocks, from_rows, 0, unroll=4)


def plane_call(recv, potential, columns, cosine, sine):
    freqs = cosine.shape[1]
    tables = plane_tables(cosine, sine)
    wide_v = tables[3].shape[1] // 2
    chunk = 1024
    vmem = pl.BlockSpec(memory_space=pltpu.VMEM)
    anywhere = pl.BlockSpec(memory_space=pl.ANY)
    along_v = columns % freqs
    along_u = columns // freqs
    along_u = along_u % 2 * (freqs // 2) + along_u // 2
    return pl.pallas_call(
        plane_kernel,
        out_shape=jax.ShapeDtypeStruct(recv.shape, jnp.float32),
        in_specs=[anywhere, vmem] + [anywhere] * 5,
        out_specs=vmem,
        scratch_shapes=[
            pltpu.VMEM((columns.shape[0], LANES), jnp.float32),
            pltpu.VMEM((freqs * freqs, LANES), jnp.float32),
            pltpu.VMEM((wide_v // LANES, freqs * ROWS, LANES), jnp.float32),
            pltpu.VMEM((wide_v // LANES, ROWS * freqs, LANES), jnp.float32),
            pltpu.VMEM(potential.shape, jnp.float32),
            *[pltpu.VMEM(table.shape, jnp.bfloat16) for table in tables],
            pltpu.SMEM((2 * chunk,), jnp.int32),
            pltpu.SemaphoreType.DMA((5,)),
            pltpu.SemaphoreType.DMA((2,)),
        ],
        compiler_params=pltpu.CompilerParams(vmem_limit_bytes=60 * 1024 * 1024),
        name="planes",
    )(along_u * freqs + along_v, recv, potential, *tables)


def greet(position, count):
    barrier = pltpu.get_barrier_semaphore()

    def signal(k, _):
        pl.semaphore_signal(barrier, inc=1, device_id={"fft": lax.rem(position + k, count)}, device_id_type=MESH)
        return 0

    lax.fori_loop(1, count, signal, 0)
    return barrier


def await_others(buffer, semaphore):
    others = buffer.at[pl.ds(0, buffer.shape[0] - 1)]
    pltpu.make_async_copy(others, others, semaphore).wait()


def start_loads(pairs, semaphore):
    loads = [pltpu.make_async_copy(source, target, semaphore.at[k]) for k, (source, target) in enumerate(pairs)]
    for load in loads:
        load.start()
    return loads


def spread_kernel(
    psi_hbm,
    high_hbm,
    low_hbm,
    recv,
    psi,
    table_high,
    table_low,
    staged,
    send,
    load_sem,
    send_sem,
    recv_sem,
):
    count, pieces, depth, _ = recv.shape
    values = pieces * depth // 2
    position = lax.axis_index("fft")
    loads = start_loads(((psi_hbm, psi), (high_hbm, table_high), (low_hbm, table_low)), load_sem)
    barrier = greet(position, count)
    for load in loads:
        load.wait()
    high, low = split(psi[...])
    staged[...] = dot(table_high[...], high) + dot(table_low[...], high) + dot(table_high[...], low)
    pl.semaphore_wait(barrier, count - 1)

    def stage(peer):
        rows = staged[pl.ds(peer * ROWS, ROWS), :]
        block = jnp.concatenate([rows[:values, :LANES], rows[:values, LANES:]], axis=0)
        return [block[k * depth : (k + 1) * depth] for k in range(pieces)]

    def post(k, _):
        peer = lax.rem(position + k, count)
        for at, piece in enumerate(stage(peer)):
            send[peer, at] = piece
        pltpu.make_async_remote_copy(
            src_ref=send.at[peer],
            dst_ref=recv.at[position],
            send_sem=send_sem,
            recv_sem=recv_sem,
            device_id={"fft": peer},
            device_id_type=MESH,
        ).start()
        return 0

    lax.fori_loop(1, count, post, 0)
    for at, piece in enumerate(stage(position)):
        recv[position, at] = piece
    await_others(recv, recv_sem)
    await_others(recv, send_sem)


def spread_call(psi, table, count, planes_held):
    rows = table.shape[0]
    vmem = pl.BlockSpec(memory_space=pltpu.VMEM)
    shape = (count, planes_held, 2 * psi.shape[1] // LANES, LANES)
    return pl.pallas_call(
        spread_kernel,
        out_shape=jax.ShapeDtypeStruct(shape, jnp.float32),
        in_specs=[pl.BlockSpec(memory_space=pl.ANY)] * 3,
        out_specs=vmem,
        scratch_shapes=[
            pltpu.VMEM(psi.shape, jnp.float32),
            pltpu.VMEM(table.shape, jnp.bfloat16),
            pltpu.VMEM(table.shape, jnp.bfloat16),
            pltpu.VMEM((rows, psi.shape[1]), jnp.float32),
            pltpu.VMEM(shape, jnp.float32),
            pltpu.SemaphoreType.DMA((3,)),
            pltpu.SemaphoreType.DMA,
            pltpu.SemaphoreType.DMA,
        ],
        compiler_params=pltpu.CompilerParams(
            collective_id=0, has_side_effects=True, vmem_limit_bytes=60 * 1024 * 1024
        ),
        name="spread",
    )(psi, *halves(table))


def collect_kernel(
    scale,
    weight,
    picked,
    columns,
    psi_hbm,
    *rest,
):
    bands = lax.axis_size("band")
    other_hbm, rest = rest[: bands - 1], rest[bands - 1 :]
    (
        high_hbm,
        low_hbm,
        hpsi,
        margin,
        psi,
        others,
        table_high,
        table_low,
        got,
        right,
        sums,
        load_sem,
        send_sem,
        recv_sem,
        sum_send_sem,
        sum_recv_sem,
    ) = rest
    count, pieces, depth, _ = picked.shape
    values = pieces * depth // 2
    freqs = hpsi.shape[2]
    position = lax.axis_index("fft")
    own = lax.axis_index("band")
    pairs = [(psi_hbm, psi), (high_hbm, table_high), (low_hbm, table_low)]
    pairs += [(source, others.at[k]) for k, source in enumerate(other_hbm)]
    loads = start_loads(pairs, load_sem)
    barrier = greet(position, count)
    pl.semaphore_wait(barrier, count - 1)

    def post(k, _):
        peer = lax.rem(position + k, count)
        pltpu.make_async_remote_copy(
            src_ref=picked.at[peer],
            dst_ref=got.at[position],
            send_sem=send_sem,
            recv_sem=recv_sem,
            device_id={"fft": peer},
            device_id_type=MESH,
        ).start()
        return 0

    lax.fori_loop(1, count, post, 0)
    got[position] = picked[position]
    for load in loads:
        load.wait()
    mine = columns[pl.ds(position * 2, 2), :]
    mine = jnp.concatenate([mine[0:1], mine[1:2]], axis=1)
    centre = freqs // 2
    along_u = jnp.floor((mine.astype(jnp.float32) + 0.5) * (1.0 / freqs)).astype(jnp.int32)
    along_v = mine - along_u * freqs - centre
    along_u = along_u - centre
    along_w = lax.broadcasted_iota(jnp.int32, (freqs, mine.shape[1]), 0) - centre
    squared = along_w * along_w + (along_u * along_u + along_v * along_v)
    kinetic = squared.astype(jnp.float32) * (0.5 / float(centre * centre))
    await_others(got, recv_sem)

    def to_right(i, _):
        block = jnp.concatenate([got[i, k] for k in range(pieces)], axis=0)
        blank = jnp.zeros((ROWS - values, LANES), jnp.float32)
        at = pl.multiple_of(i * ROWS, ROWS)
        right[pl.ds(at, ROWS), 0:LANES] = jnp.concatenate([block[:values], blank], axis=0)
        right[pl.ds(at, ROWS), LANES : 2 * LANES] = jnp.concatenate([block[values:], blank], axis=0)
        return 0

    lax.fori_loop(0, count, to_right, 0, unroll=4)
    high, low = split(right[...])
    applied = dot(table_high[...], high) + dot(table_low[...], high) + dot(table_high[...], low)
    right_re = kinetic * psi[0:freqs, :] + applied[:freqs] * scale
    right_im = kinetic * psi[freqs : 2 * freqs, :] + applied[freqs:] * scale
    hpsi[0, 0] = right_re
    hpsi[1, 0] = right_im

    def folded(product):
        narrow = product[:, :LANES] + product[:, LANES:]
        return jnp.sum(narrow, axis=0, keepdims=True)

    line = lax.broadcasted_iota(jnp.int32, (2 * bands, LANES), 0)
    tile = jnp.zeros((2 * bands, LANES), jnp.float32)
    for k in range(bands):
        left = psi if k == 0 else others.at[k - 1]
        left_re, left_im = left[0:freqs, :], left[freqs : 2 * freqs, :]
        row = lax.rem(own + k, bands)
        tile = jnp.where(line == row, folded(left_re * right_re + left_im * right_im), tile)
        tile = jnp.where(line == row + bands, folded(left_re * right_im - left_im * right_re), tile)
    sums[position] = tile * weight

    def post_sums(k, _):
        pltpu.make_async_remote_copy(
            src_ref=sums.at[position],
            dst_ref=sums.at[position],
            send_sem=sum_send_sem,
            recv_sem=sum_recv_sem,
            device_id={"fft": lax.rem(position + k, count)},
            device_id_type=MESH,
        ).start()
        return 0

    lax.fori_loop(1, count, post_sums, 0)
    await_others(sums, sum_recv_sem)
    margin[...] = jnp.sum(jnp.sum(sums[...], axis=0), axis=1, keepdims=True)
    await_others(got, send_sem)
    await_others(sums, sum_send_sem)


def collect_call(picked, columns, psi, others, table, scale, weight, shape):
    count = picked.shape[0]
    vmem = pl.BlockSpec(memory_space=pltpu.VMEM)
    anywhere = pl.BlockSpec(memory_space=pl.ANY)
    height = 2 * (len(others) + 1)
    table = table.T
    return pl.pallas_call(
        functools.partial(collect_kernel, scale, weight),
        out_shape=(jax.ShapeDtypeStruct(shape, jnp.float32), jax.ShapeDtypeStruct((height, 1), jnp.float32)),
        in_specs=[vmem] * 2 + [anywhere] * (3 + len(others)),
        out_specs=(vmem, vmem),
        scratch_shapes=[
            pltpu.VMEM(psi.shape, jnp.float32),
            pltpu.VMEM((len(others), *psi.shape), jnp.float32),
            pltpu.VMEM(table.shape, jnp.bfloat16),
            pltpu.VMEM(table.shape, jnp.bfloat16),
            pltpu.VMEM(picked.shape, jnp.float32),
            pltpu.VMEM((count * ROWS, psi.shape[1]), jnp.float32),
            pltpu.VMEM((count, height, LANES), jnp.float32),
            pltpu.SemaphoreType.DMA((3 + len(others),)),
            pltpu.SemaphoreType.DMA,
            pltpu.SemaphoreType.DMA,
            pltpu.SemaphoreType.DMA,
            pltpu.SemaphoreType.DMA,
        ],
        compiler_params=pltpu.CompilerParams(
            collective_id=1, has_side_effects=True, vmem_limit_bytes=60 * 1024 * 1024
        ),
        name="collect",
    )(picked, columns.reshape(-1, LANES), psi, *others, *halves(table))


def on_device(psi, potential, stick_columns):
    freq_count = psi.shape[2]
    per_device = psi.shape[3]
    grid_size = potential.shape[1]
    plane_count = potential.shape[0]
    fft_count = lax.axis_size("fft")
    cosine, sine = dft_tables(grid_size, freq_count)
    table = np.stack([np.concatenate([cosine, -sine], 1), np.concatenate([sine, cosine], 1)])
    table = table.reshape(2, fft_count, plane_count, 2 * freq_count).transpose(1, 0, 2, 3)
    table = table.reshape(fft_count, 2 * plane_count, 2 * freq_count)
    table = np.pad(table, ((0, 0), (0, ROWS - 2 * plane_count), (0, 0))).reshape(fft_count * ROWS, 2 * freq_count)
    flat_psi = psi.reshape(2 * freq_count, per_device)
    moved = spread_call(flat_psi, table, fft_count, plane_count)
    bands = lax.axis_size("band")
    held, moved = lax.optimization_barrier((flat_psi, moved))
    others = [
        lax.ppermute(held, "band", [((i + k) % bands, i) for i in range(bands)]) for k in range(1, bands)
    ]
    picked = plane_call(moved, potential, stick_columns, cosine, sine)
    scale = 1.0 / float(grid_size * grid_size * grid_size)
    weight = 1.0 / float(freq_count * per_device * fft_count)
    hpsi, margin = collect_call(picked, stick_columns, flat_psi, others, table, scale, weight, psi.shape)
    return (hpsi, margin.reshape(2, bands, 1))


def solution(mesh):
    placed = (P(None, "band", None, "fft"), P("fft", None, None), P())
    return jax.shard_map(
        on_device,
        mesh=mesh,
        in_specs=placed,
        out_specs=(P(None, "band", None, "fft"), P(None, None, "band")),
        check_vma=False,
    )
```

```python
import functools
import math

import jax
import jax.numpy as jnp
import numpy as np
from jax import lax
from jax.experimental import pallas as pl
from jax.experimental.pallas import tpu as pltpu
from jax.sharding import PartitionSpec as P

LANES = 128
ROWS = 16
MESH = pl.DeviceIdType.MESH


def dft_tables(grid_size, freq_count):
    points = np.arange(grid_size)[:, None]
    freqs = np.arange(freq_count)[None, :] - freq_count // 2
    angle = (points * freqs % grid_size).astype(np.float64) * (2.0 * math.pi / grid_size)
    return np.cos(angle).astype(np.float32), np.sin(angle).astype(np.float32)


def halves(table):
    high = table.astype(jnp.bfloat16)
    low = (table - high.astype(np.float32)).astype(jnp.bfloat16)
    return high, low


def split(value):
    high = value.astype(jnp.bfloat16)
    low = (value - high.astype(jnp.float32)).astype(jnp.bfloat16)
    return high, low


def dot(left, right):
    return jnp.dot(left, right, preferred_element_type=jnp.float32)


def packed_rows(table, whole):
    high, low = halves(table)
    tail = table.shape[0] - whole
    spare = np.zeros((-3 * tail % LANES, table.shape[1]), high.dtype)
    if whole % (2 * LANES) == 0:
        spare = np.zeros((-3 * tail % (2 * LANES), table.shape[1]), high.dtype)
    return np.concatenate([high[:whole], high[:whole], low[:whole], high[whole:], high[whole:], low[whole:], spare], axis=0)


def packed_columns(value, whole, tail):
    high, low = split(value)
    rest_high = high[:, whole : whole + LANES].astype(jnp.float32)
    rest_low = low[:, whole : whole + LANES].astype(jnp.float32)
    parts = [high[:, :whole], low[:, :whole], high[:, :whole]]
    if 3 * tail <= LANES:
        rest = rest_high + pltpu.roll(rest_low, tail, 1) + pltpu.roll(rest_high, 2 * tail, 1)
        parts.append(rest.astype(jnp.bfloat16))
    else:
        parts.append((rest_high + pltpu.roll(rest_low, tail, 1)).astype(jnp.bfloat16))
        parts.append(rest_high.astype(jnp.bfloat16))
    return jnp.concatenate(parts, axis=1)


def three(table):
    high, low = halves(table)
    return np.concatenate([high, low, high], axis=1)


def whole_lanes(count):
    return count // LANES * LANES


def plane_tables(cosine, sine):
    grid, freqs = cosine.shape
    half = grid // 2
    wide = -(-grid // LANES) * LANES
    wide_v = -(-freqs // LANES) * LANES
    y_out = np.zeros((freqs, 2 * wide), np.float32)
    y_out[:, :grid] = cosine.T
    y_out[:, wide : wide + grid] = sine.T
    y_back = np.zeros((grid, 2 * wide_v), np.float32)
    y_back[:, :freqs] = cosine
    y_back[:, wide_v : wide_v + freqs] = sine
    x_out = [three(np.concatenate([cosine[:half, k::2], sine[:half, k::2]], axis=0)) for k in (0, 1)]
    x_back = [three(np.concatenate([cosine[:half, k::2].T, sine[:half, k::2].T], axis=0)) for k in (0, 1)]
    return (
        packed_rows(y_out, whole_lanes(freqs)),
        np.stack(x_out),
        np.stack(x_back),
        packed_rows(y_back, whole_lanes(grid)),
    )


def stacked(value):
    high, low = split(value)
    return jnp.concatenate([high, high, low], axis=0)


def complex_parts(prod, rows, wide, sign):
    real = prod[:rows, :wide] - sign * prod[rows:, wide:]
    imag = prod[:rows, wide:] + sign * prod[rows:, :wide]
    return real, imag


def walk(columns, index, index_sem, visit, first=0):
    chunk = index.shape[0] // 2
    pairs = columns.shape[0] // (2 * chunk)

    def fetch(step, slot):
        number = lax.rem(first + step, 2 * pairs)
        source = columns.at[pl.ds(pl.multiple_of(number * chunk, chunk), chunk)]
        return pltpu.make_async_copy(source, index.at[pl.ds(slot * chunk, chunk)], index_sem.at[slot])

    fetch(0, 0).start()

    def pair(i, _):
        fetch(2 * i + 1, 1).start()
        fetch(2 * i, 0).wait()
        visit(lax.rem(first + 2 * i, 2 * pairs), 0, chunk)

        @pl.when(i < pairs - 1)
        def _():
            fetch(2 * i + 2, 0).start()

        fetch(2 * i + 1, 1).wait()
        visit(lax.rem(first + 2 * i + 1, 2 * pairs), chunk, chunk)
        return 0

    lax.fori_loop(0, pairs, pair, 0)


def through_planes(flat, planes, potential, y_out, x_out, x_back, y_back):
    planes_held, grid, _ = potential.shape
    half = grid // 2
    freqs = x_back.shape[1]
    even = freqs // 2
    wide = y_out.shape[1] // 2
    wide_v = y_back.shape[1] // 2

    def plane(z, _):
        lane = lax.broadcasted_iota(jnp.int32, (2 * freqs, LANES), 1)
        tiles = []
        for k in range(flat.shape[0]):
            pair = [flat[k, pl.ds(at, freqs, stride=ROWS), :] for at in (z, planes_held + z)]
            pair = jnp.concatenate(pair, axis=0)
            tiles.append(pair if freqs - k * LANES >= LANES else jnp.where(lane < freqs - k * LANES, pair, 0.0))
        left = packed_columns(jnp.concatenate(tiles, axis=1), whole_lanes(freqs), freqs % LANES)
        along = jnp.concatenate(complex_parts(dot(left, y_out[...]), freqs, wide, 1.0), axis=1)
        first_re, first_im = complex_parts(dot(x_out[0], stacked(along[:even])), half, wide, 1.0)
        second_re, second_im = complex_parts(dot(x_out[1], stacked(along[even:])), half, wide, 1.0)
        lower = potential[z, 0:half, :]
        upper = potential[z, half:grid, :]
        blank = jnp.zeros((half, wide - grid), jnp.float32)
        lower = jnp.concatenate([lower, blank], axis=1)
        upper = jnp.concatenate([upper, blank], axis=1)
        low_re, low_im = (first_re + second_re) * lower, (first_im + second_im) * lower
        up_re, up_im = (first_re - second_re) * upper, (first_im - second_im) * upper
        added = jnp.concatenate([low_re + up_re, low_im + up_im], axis=1)
        taken = jnp.concatenate([low_re - up_re, low_im - up_im], axis=1)
        even_re, even_im = complex_parts(dot(x_back[0], stacked(added)), even, wide, -1.0)
        odd_re, odd_im = complex_parts(dot(x_back[1], stacked(taken)), even, wide, -1.0)
        left = packed_columns(
            jnp.concatenate([even_re, odd_re, even_im, odd_im], axis=0), whole_lanes(grid), grid % LANES
        )
        prod = dot(left, y_back[...])
        done_re = prod[:freqs, :wide_v] + prod[freqs:, wide_v:]
        done_im = prod[freqs:, :wide_v] - prod[:freqs, wide_v:]
        for k in range(planes.shape[0]):
            planes[k, pl.ds(z * freqs, freqs), :] = done_re[:, k * LANES : (k + 1) * LANES]
            planes[k, pl.ds((planes_held + z) * freqs, freqs), :] = done_im[:, k * LANES : (k + 1) * LANES]
        return 0

    lax.fori_loop(0, planes_held, plane, 0)


def start_loads(pairs, semaphore):
    loads = [pltpu.make_async_copy(source, target, semaphore.at[k]) for k, (source, target) in enumerate(pairs)]
    for load in loads:
        load.start()
    return loads


def place_kernel(columns, recv, flat, sticks, grid_rows, index, index_sem):
    blocks, pieces, depth, _ = recv.shape
    values = pieces * depth // 2
    freqs = flat.shape[1] // ROWS
    batch = 64

    def clear(i, _):
        grid_rows[pl.ds(i * freqs, freqs), :] = jnp.zeros((freqs, LANES), jnp.float32)
        return 0

    lax.fori_loop(0, freqs, clear, 0)

    def to_rows(i, _):
        block = jnp.concatenate([recv[i, k] for k in range(pieces)], axis=0)
        block = jnp.concatenate([block, jnp.zeros((LANES - block.shape[0], LANES), jnp.float32)], axis=0)
        turned = block.T
        sticks[pl.ds(i * 2 * LANES, LANES), :] = turned
        sticks[pl.ds(i * 2 * LANES + LANES, LANES), :] = pltpu.roll(turned, LANES - values, 1)
        return 0

    lax.fori_loop(0, blocks, to_rows, 0, unroll=4)

    def scatter(number, offset, count):
        base = pl.multiple_of(number * count, count)
        for k in range(0, count, batch):
            rows = [sticks[pl.ds(base + k + j, 1), :] for j in range(batch)]
            for j in range(batch):
                grid_rows[pl.ds(index[offset + k + j], 1), :] = rows[j]

    walk(columns, index, index_sem, scatter)

    def to_planes(u, _):
        turned = grid_rows[pl.ds(u * freqs, freqs), :].T
        for k in range(flat.shape[0]):
            upper = min(freqs - k * LANES, LANES)
            flat[k, pl.ds(u * ROWS, ROWS), 0:upper] = turned[0:ROWS, k * LANES : k * LANES + upper]
        return 0

    lax.fori_loop(0, freqs, to_planes, 0, unroll=8)


def place_call(recv, columns, freqs):
    chunk = 1024
    tiles = -(-freqs // LANES)
    vmem = pl.BlockSpec(memory_space=pltpu.VMEM)
    anywhere = pl.BlockSpec(memory_space=pl.ANY)
    return pl.pallas_call(
        place_kernel,
        out_shape=jax.ShapeDtypeStruct((tiles, freqs * ROWS, LANES), jnp.float32),
        in_specs=[anywhere, vmem],
        out_specs=vmem,
        scratch_shapes=[
            pltpu.VMEM((columns.shape[0], LANES), jnp.float32),
            pltpu.VMEM((freqs * freqs, LANES), jnp.float32),
            pltpu.SMEM((2 * chunk,), jnp.int32),
            pltpu.SemaphoreType.DMA((2,)),
        ],
        compiler_params=pltpu.CompilerParams(vmem_limit_bytes=60 * 1024 * 1024),
        name="place",
    )(columns, recv)


def greet(position, count, own=None, bands=1):
    barrier = pltpu.get_barrier_semaphore()
    for k in range(1, bands):
        pl.semaphore_signal(barrier, inc=1, device_id={"band": lax.rem(own + k, bands)}, device_id_type=MESH)

    def signal(k, _):
        pl.semaphore_signal(barrier, inc=1, device_id={"fft": lax.rem(position + k, count)}, device_id_type=MESH)
        return 0

    lax.fori_loop(1, count, signal, 0)
    return barrier


def await_others(buffer, semaphore):
    others = buffer.at[pl.ds(0, buffer.shape[0] - 1)]
    pltpu.make_async_copy(others, others, semaphore).wait()


def spread_kernel(
    psi_hbm,
    high_hbm,
    low_hbm,
    recv,
    psi,
    table_high,
    table_low,
    staged,
    send,
    load_sem,
    send_sem,
    recv_sem,
):
    count, pieces, depth, _ = recv.shape
    values = pieces * depth // 2
    position = lax.axis_index("fft")
    loads = start_loads(((psi_hbm, psi), (high_hbm, table_high), (low_hbm, table_low)), load_sem)
    barrier = greet(position, count)
    for load in loads:
        load.wait()
    high, low = split(psi[...])
    staged[...] = dot(table_high[...], high) + dot(table_low[...], high) + dot(table_high[...], low)
    pl.semaphore_wait(barrier, count - 1)

    def stage(peer):
        rows = staged[pl.ds(peer * ROWS, ROWS), :]
        block = jnp.concatenate([rows[:values, :LANES], rows[:values, LANES:]], axis=0)
        return [block[k * depth : (k + 1) * depth] for k in range(pieces)]

    def post(k, _):
        peer = lax.rem(position + k, count)
        for at, piece in enumerate(stage(peer)):
            send[peer, at] = piece
        pltpu.make_async_remote_copy(
            src_ref=send.at[peer],
            dst_ref=recv.at[position],
            send_sem=send_sem,
            recv_sem=recv_sem,
            device_id={"fft": peer},
            device_id_type=MESH,
        ).start()
        return 0

    lax.fori_loop(1, count, post, 0)
    for at, piece in enumerate(stage(position)):
        recv[position, at] = piece
    await_others(recv, recv_sem)
    await_others(recv, send_sem)


def spread_call(psi, table, count, planes_held):
    rows = table.shape[0]
    vmem = pl.BlockSpec(memory_space=pltpu.VMEM)
    shape = (count, planes_held, 2 * psi.shape[1] // LANES, LANES)
    return pl.pallas_call(
        spread_kernel,
        out_shape=jax.ShapeDtypeStruct(shape, jnp.float32),
        in_specs=[pl.BlockSpec(memory_space=pl.ANY)] * 3,
        out_specs=vmem,
        scratch_shapes=[
            pltpu.VMEM(psi.shape, jnp.float32),
            pltpu.VMEM(table.shape, jnp.bfloat16),
            pltpu.VMEM(table.shape, jnp.bfloat16),
            pltpu.VMEM((rows, psi.shape[1]), jnp.float32),
            pltpu.VMEM(shape, jnp.float32),
            pltpu.SemaphoreType.DMA((3,)),
            pltpu.SemaphoreType.DMA,
            pltpu.SemaphoreType.DMA,
        ],
        compiler_params=pltpu.CompilerParams(
            collective_id=0, has_side_effects=True, vmem_limit_bytes=60 * 1024 * 1024
        ),
        name="spread",
    )(psi, *halves(table))


def collect_kernel(
    scale,
    weight,
    index_hbm,
    columns,
    psi_hbm,
    flat_hbm,
    potential_hbm,
    high_hbm,
    low_hbm,
    y_out_hbm,
    x_out_hbm,
    x_back_hbm,
    y_back_hbm,
    hpsi,
    margin,
    psi,
    flat,
    potential,
    table_high,
    table_low,
    y_out,
    x_out,
    x_back,
    y_back,
    others,
    planes,
    grid_rows,
    sticks,
    send,
    got,
    right,
    sums,
    index,
    index_sem,
    load_sem,
    band_send_sem,
    band_recv_sem,
    send_sem,
    recv_sem,
    sum_send_sem,
    sum_recv_sem,
):
    bands = others.shape[0] + 1
    count, pieces, depth, _ = got.shape
    values = pieces * depth // 2
    freqs = hpsi.shape[2]
    per_device = hpsi.shape[3]
    batch = 64
    position = lax.axis_index("fft")
    own = lax.axis_index("band")
    loads = start_loads(
        (
            (flat_hbm, flat),
            (y_out_hbm, y_out),
            (x_out_hbm, x_out),
            (potential_hbm, potential),
            (x_back_hbm, x_back),
            (y_back_hbm, y_back),
            (psi_hbm, psi),
            (high_hbm, table_high),
            (low_hbm, table_low),
        ),
        load_sem,
    )
    barrier = greet(position, count, own, bands)
    pl.semaphore_wait(barrier, count + bands - 2)
    band_copies = [
        pltpu.make_async_remote_copy(
            src_ref=psi_hbm,
            dst_ref=others.at[k - 1],
            send_sem=band_send_sem.at[k - 1],
            recv_sem=band_recv_sem.at[k - 1],
            device_id={"band": lax.rem(own + bands - k, bands)},
            device_id_type=MESH,
        )
        for k in range(1, bands)
    ]
    for copy in band_copies:
        copy.start()
    for load in loads:
        load.wait()
    through_planes(flat, planes, potential, y_out, x_out, x_back, y_back)

    def from_planes(u, _):
        for k in range(planes.shape[0]):
            upper = min(freqs - k * LANES, LANES)
            turned = planes[k, pl.ds(u, ROWS, stride=freqs), :].T
            grid_rows[pl.ds(u * freqs + k * LANES, upper), 0:ROWS] = turned[:upper]
        return 0

    lax.fori_loop(0, freqs, from_planes, 0, unroll=8)

    def gather(number, offset, length):
        for k in range(0, length, batch):
            rows = [grid_rows[pl.ds(index[offset + k + j], 1), :] for j in range(batch)]
            for j in range(batch):
                sticks[pl.ds(offset + k + j, 1), :] = rows[j]
        group = length // per_device
        for k in range(group):
            at = offset + k * per_device
            first = sticks[pl.ds(at, LANES), :].T[:values]
            second = sticks[pl.ds(at + LANES, LANES), :].T[:values]
            block = jnp.concatenate([first, second], axis=0)
            for piece in range(pieces):
                send[number * group + k, piece] = block[piece * depth : (piece + 1) * depth]
        for k in range(group):
            peer = number * group + k

            @pl.when(peer != position)
            def _(peer=peer):
                pltpu.make_async_remote_copy(
                    src_ref=send.at[peer],
                    dst_ref=got.at[position],
                    send_sem=send_sem,
                    recv_sem=recv_sem,
                    device_id={"fft": peer},
                    device_id_type=MESH,
                ).start()

    chunk = index.shape[0] // 2
    walk(index_hbm, index, index_sem, gather, lax.div(position * per_device, chunk) + 1)
    got[position] = send[position]
    mine = columns[pl.ds(position * 2, 2), :]
    mine = jnp.concatenate([mine[0:1], mine[1:2]], axis=1)
    centre = freqs // 2
    along_u = jnp.floor((mine.astype(jnp.float32) + 0.5) * (1.0 / freqs)).astype(jnp.int32)
    along_v = mine - along_u * freqs - centre
    along_u = along_u - centre
    along_w = lax.broadcasted_iota(jnp.int32, (freqs, mine.shape[1]), 0) - centre
    squared = along_w * along_w + (along_u * along_u + along_v * along_v)
    kinetic = squared.astype(jnp.float32) * (0.5 / float(centre * centre))
    await_others(got, recv_sem)

    def to_right(i, _):
        block = jnp.concatenate([got[i, k] for k in range(pieces)], axis=0)
        blank = jnp.zeros((ROWS - values, LANES), jnp.float32)
        at = pl.multiple_of(i * ROWS, ROWS)
        right[pl.ds(at, ROWS), 0:LANES] = jnp.concatenate([block[:values], blank], axis=0)
        right[pl.ds(at, ROWS), LANES : 2 * LANES] = jnp.concatenate([block[values:], blank], axis=0)
        return 0

    lax.fori_loop(0, count, to_right, 0, unroll=4)
    high, low = split(right[...])
    applied = dot(table_high[...], high) + dot(table_low[...], high) + dot(table_high[...], low)
    right_re = kinetic * psi[0:freqs, :] + applied[:freqs] * scale
    right_im = kinetic * psi[freqs : 2 * freqs, :] + applied[freqs:] * scale
    hpsi[0, 0] = right_re
    hpsi[1, 0] = right_im

    def folded(product):
        narrow = product[:, :LANES] + product[:, LANES:]
        return jnp.sum(narrow, axis=0, keepdims=True)

    for copy in band_copies:
        copy.wait()
    line = lax.broadcasted_iota(jnp.int32, (2 * bands, LANES), 0)
    tile = jnp.zeros((2 * bands, LANES), jnp.float32)
    for k in range(bands):
        left = psi if k == 0 else others.at[k - 1]
        left_re, left_im = left[0:freqs, :], left[freqs : 2 * freqs, :]
        row = lax.rem(own + k, bands)
        tile = jnp.where(line == row, folded(left_re * right_re + left_im * right_im), tile)
        tile = jnp.where(line == row + bands, folded(left_re * right_im - left_im * right_re), tile)
    sums[position] = tile * weight

    def post_sums(k, _):
        pltpu.make_async_remote_copy(
            src_ref=sums.at[position],
            dst_ref=sums.at[position],
            send_sem=sum_send_sem,
            recv_sem=sum_recv_sem,
            device_id={"fft": lax.rem(position + k, count)},
            device_id_type=MESH,
        ).start()
        return 0

    lax.fori_loop(1, count, post_sums, 0)
    await_others(sums, sum_recv_sem)
    margin[...] = jnp.sum(jnp.sum(sums[...], axis=0), axis=1, keepdims=True)
    await_others(got, send_sem)
    await_others(sums, sum_send_sem)


def collect_call(flat, potential, renumbered, columns, psi, table, cosine, sine, scale, weight, shape, count, bands):
    freqs = cosine.shape[1]
    planes_held = potential.shape[0]
    vmem = pl.BlockSpec(memory_space=pltpu.VMEM)
    anywhere = pl.BlockSpec(memory_space=pl.ANY)
    chunk = 1024
    table = table.T
    tables = plane_tables(cosine, sine)
    blocks = (count, planes_held, 2 * psi.shape[1] // LANES, LANES)
    operands = (psi, flat, potential, *halves(table), *tables)
    return pl.pallas_call(
        functools.partial(collect_kernel, scale, weight),
        out_shape=(jax.ShapeDtypeStruct(shape, jnp.float32), jax.ShapeDtypeStruct((2 * bands, 1), jnp.float32)),
        in_specs=[anywhere, vmem] + [anywhere] * len(operands),
        out_specs=(vmem, vmem),
        scratch_shapes=[
            *[pltpu.VMEM(operand.shape, operand.dtype) for operand in operands],
            pltpu.VMEM((bands - 1, *psi.shape), jnp.float32),
            pltpu.VMEM((flat.shape[0], ROWS * freqs, LANES), jnp.float32),
            pltpu.VMEM((freqs * freqs, LANES), jnp.float32),
            pltpu.VMEM((2 * chunk, LANES), jnp.float32),
            pltpu.VMEM(blocks, jnp.float32),
            pltpu.VMEM(blocks, jnp.float32),
            pltpu.VMEM((count * ROWS, psi.shape[1]), jnp.float32),
            pltpu.VMEM((count, 2 * bands, LANES), jnp.float32),
            pltpu.SMEM((2 * chunk,), jnp.int32),
            pltpu.SemaphoreType.DMA((2,)),
            pltpu.SemaphoreType.DMA((len(operands),)),
            pltpu.SemaphoreType.DMA((bands - 1,)),
            pltpu.SemaphoreType.DMA((bands - 1,)),
            pltpu.SemaphoreType.DMA,
            pltpu.SemaphoreType.DMA,
            pltpu.SemaphoreType.DMA,
            pltpu.SemaphoreType.DMA,
        ],
        compiler_params=pltpu.CompilerParams(
            collective_id=1, has_side_effects=True, vmem_limit_bytes=60 * 1024 * 1024
        ),
        name="collect",
    )(renumbered, columns.reshape(-1, LANES), *operands)


def on_device(psi, potential, stick_columns):
    freq_count = psi.shape[2]
    per_device = psi.shape[3]
    grid_size = potential.shape[1]
    plane_count = potential.shape[0]
    fft_count = lax.axis_size("fft")
    cosine, sine = dft_tables(grid_size, freq_count)
    table = np.stack([np.concatenate([cosine, -sine], 1), np.concatenate([sine, cosine], 1)])
    table = table.reshape(2, fft_count, plane_count, 2 * freq_count).transpose(1, 0, 2, 3)
    table = table.reshape(fft_count, 2 * plane_count, 2 * freq_count)
    table = np.pad(table, ((0, 0), (0, ROWS - 2 * plane_count), (0, 0))).reshape(fft_count * ROWS, 2 * freq_count)
    flat_psi = psi.reshape(2 * freq_count, per_device)
    moved = spread_call(flat_psi, table, fft_count, plane_count)
    bands = lax.axis_size("band")
    along_v = stick_columns % freq_count
    along_u = stick_columns // freq_count
    along_u = along_u % 2 * (freq_count // 2) + along_u // 2
    renumbered = along_u * freq_count + along_v
    flat = place_call(moved, renumbered, freq_count)
    scale = 1.0 / float(grid_size * grid_size * grid_size)
    weight = 1.0 / float(freq_count * per_device * fft_count)
    hpsi, margin = collect_call(
        flat,
        potential,
        renumbered,
        stick_columns,
        flat_psi,
        table,
        cosine,
        sine,
        scale,
        weight,
        psi.shape,
        fft_count,
        bands,
    )
    return (hpsi, margin.reshape(2, bands, 1))


def solution(mesh):
    placed = (P(None, "band", None, "fft"), P("fft", None, None), P())
    return jax.shard_map(
        on_device,
        mesh=mesh,
        in_specs=placed,
        out_specs=(P(None, "band", None, "fft"), P(None, None, "band")),
        check_vma=False,
    )
```

```python
import functools
import math

import jax
import jax.numpy as jnp
import numpy as np
from jax import lax
from jax.experimental import pallas as pl
from jax.experimental.pallas import tpu as pltpu
from jax.sharding import PartitionSpec as P

LANES = 128
ROWS = 16
PACK = 4
CHUNK = 1024
MESH = pl.DeviceIdType.MESH


def dft_tables(grid_size, freq_count):
    points = np.arange(grid_size)[:, None]
    freqs = np.arange(freq_count)[None, :] - freq_count // 2
    angle = (points * freqs % grid_size).astype(np.float64) * (2.0 * math.pi / grid_size)
    return np.cos(angle).astype(np.float32), np.sin(angle).astype(np.float32)


def halves(table):
    high = table.astype(jnp.bfloat16)
    low = (table - high.astype(np.float32)).astype(jnp.bfloat16)
    return high, low


def split(value):
    high = value.astype(jnp.bfloat16)
    low = (value - high.astype(jnp.float32)).astype(jnp.bfloat16)
    return high, low


def dot(left, right):
    return jnp.dot(left, right, preferred_element_type=jnp.float32)


def packed_rows(table, whole):
    high, low = halves(table)
    tail = table.shape[0] - whole
    spare = np.zeros((-3 * tail % LANES, table.shape[1]), high.dtype)
    if whole % (2 * LANES) == 0:
        spare = np.zeros((-3 * tail % (2 * LANES), table.shape[1]), high.dtype)
    return np.concatenate([high[:whole], high[:whole], low[:whole], high[whole:], high[whole:], low[whole:], spare], axis=0)


def packed_columns(value, whole, tail):
    high, low = split(value)
    rest_high = high[:, whole : whole + LANES].astype(jnp.float32)
    rest_low = low[:, whole : whole + LANES].astype(jnp.float32)
    parts = [high[:, :whole], low[:, :whole], high[:, :whole]]
    if 3 * tail <= LANES:
        rest = rest_high + pltpu.roll(rest_low, tail, 1) + pltpu.roll(rest_high, 2 * tail, 1)
        parts.append(rest.astype(jnp.bfloat16))
    else:
        parts.append((rest_high + pltpu.roll(rest_low, tail, 1)).astype(jnp.bfloat16))
        parts.append(rest_high.astype(jnp.bfloat16))
    return jnp.concatenate(parts, axis=1)


def three(table):
    high, low = halves(table)
    return np.concatenate([high, low, high], axis=1)


def whole_lanes(count):
    return count // LANES * LANES


def plane_tables(cosine, sine):
    grid, freqs = cosine.shape
    half = grid // 2
    wide = -(-grid // LANES) * LANES
    wide_v = -(-freqs // LANES) * LANES
    y_out = np.zeros((freqs, 2 * wide), np.float32)
    y_out[:, :grid] = cosine.T
    y_out[:, wide : wide + grid] = sine.T
    y_back = np.zeros((grid, 2 * wide_v), np.float32)
    y_back[:, :freqs] = cosine
    y_back[:, wide_v : wide_v + freqs] = sine
    x_out = [three(np.concatenate([cosine[:half, k::2], sine[:half, k::2]], axis=0)) for k in (0, 1)]
    x_back = [three(np.concatenate([cosine[:half, k::2].T, sine[:half, k::2].T], axis=0)) for k in (0, 1)]
    return (
        packed_rows(y_out, whole_lanes(freqs)),
        np.stack(x_out),
        np.stack(x_back),
        packed_rows(y_back, whole_lanes(grid)),
    )


def stacked(value):
    high, low = split(value)
    return jnp.concatenate([high, high, low], axis=0)


def complex_parts(prod, rows, wide, sign):
    real = prod[:rows, :wide] - sign * prod[rows:, wide:]
    imag = prod[:rows, wide:] + sign * prod[rows:, :wide]
    return real, imag


def walk(columns, index, index_sem, visit, first=0):
    steps = columns.shape[0] // CHUNK

    def number_of(step):
        return lax.rem(first + step, steps)

    def fetch(step, slot):
        source = columns.at[pl.ds(pl.multiple_of(number_of(step) * CHUNK, CHUNK), CHUNK)]
        return pltpu.make_async_copy(source, index.at[pl.ds(slot * CHUNK, CHUNK)], index_sem.at[slot])

    fetch(0, 0).start()

    def pair(i, _):
        fetch(2 * i + 1, 1).start()
        fetch(2 * i, 0).wait()
        visit(2 * i, 0)

        @pl.when(i < steps // 2 - 1)
        def _():
            fetch(2 * i + 2, 0).start()

        fetch(2 * i + 1, 1).wait()
        visit(2 * i + 1, 1)
        return 0

    lax.fori_loop(0, steps // 2, pair, 0)


def through_planes(flat, planes, potential, y_out, x_out, x_back, y_back):
    planes_held, grid, _ = potential.shape
    half = grid // 2
    freqs = x_back.shape[1]
    even = freqs // 2
    wide = y_out.shape[1] // 2
    wide_v = y_back.shape[1] // 2

    def plane(z, _):
        lane = lax.broadcasted_iota(jnp.int32, (2 * freqs, LANES), 1)
        tiles = []
        for k in range(flat.shape[0]):
            pair = [flat[k, pl.ds(at, freqs, stride=ROWS), :] for at in (z, planes_held + z)]
            pair = jnp.concatenate(pair, axis=0)
            tiles.append(pair if freqs - k * LANES >= LANES else jnp.where(lane < freqs - k * LANES, pair, 0.0))
        left = packed_columns(jnp.concatenate(tiles, axis=1), whole_lanes(freqs), freqs % LANES)
        along = jnp.concatenate(complex_parts(dot(left, y_out[...]), freqs, wide, 1.0), axis=1)
        first_re, first_im = complex_parts(dot(x_out[0], stacked(along[:even])), half, wide, 1.0)
        second_re, second_im = complex_parts(dot(x_out[1], stacked(along[even:])), half, wide, 1.0)
        lower = potential[z, 0:half, :]
        upper = potential[z, half:grid, :]
        blank = jnp.zeros((half, wide - grid), jnp.float32)
        lower = jnp.concatenate([lower, blank], axis=1)
        upper = jnp.concatenate([upper, blank], axis=1)
        low_re, low_im = (first_re + second_re) * lower, (first_im + second_im) * lower
        up_re, up_im = (first_re - second_re) * upper, (first_im - second_im) * upper
        added = jnp.concatenate([low_re + up_re, low_im + up_im], axis=1)
        taken = jnp.concatenate([low_re - up_re, low_im - up_im], axis=1)
        even_re, even_im = complex_parts(dot(x_back[0], stacked(added)), even, wide, -1.0)
        odd_re, odd_im = complex_parts(dot(x_back[1], stacked(taken)), even, wide, -1.0)
        left = packed_columns(
            jnp.concatenate([even_re, odd_re, even_im, odd_im], axis=0), whole_lanes(grid), grid % LANES
        )
        prod = dot(left, y_back[...])
        done_re = prod[:freqs, :wide_v] + prod[freqs:, wide_v:]
        done_im = prod[freqs:, :wide_v] - prod[:freqs, wide_v:]
        for k in range(planes.shape[0]):
            planes[k, pl.ds(z * freqs, freqs), :] = done_re[:, k * LANES : (k + 1) * LANES]
            planes[k, pl.ds((planes_held + z) * freqs, freqs), :] = done_im[:, k * LANES : (k + 1) * LANES]
        return 0

    lax.fori_loop(0, planes_held, plane, 0)


def start_loads(pairs, semaphore):
    loads = [pltpu.make_async_copy(source, target, semaphore.at[k]) for k, (source, target) in enumerate(pairs)]
    for load in loads:
        load.start()
    return loads


def place_kernel(index_hbm, columns, recv, flat, kinetic, sticks, grid_rows, index, index_sem):
    blocks, pieces, depth, _ = recv.shape
    values = pieces * depth // 2
    freqs = flat.shape[1] // ROWS
    batch = 64

    def clear(i, _):
        grid_rows[pl.ds(i * freqs, freqs), :] = jnp.zeros((freqs, LANES), jnp.float32)
        return 0

    lax.fori_loop(0, freqs, clear, 0)

    per_device = 2 * LANES
    group = CHUNK // per_device
    steps = blocks // group

    def to_rows(step, slot):
        for b in range(group):
            i = lax.rem(step, steps) * group + b
            block = jnp.concatenate([recv[i, k] for k in range(pieces)], axis=0)
            block = jnp.concatenate([block, jnp.zeros((LANES - block.shape[0], LANES), jnp.float32)], axis=0)
            turned = block.T
            at = slot * CHUNK + b * per_device
            sticks[at : at + LANES, :] = turned
            sticks[at + LANES : at + per_device, :] = pltpu.roll(turned, LANES - values, 1)

    to_rows(0, 0)

    def scatter(step, slot):
        to_rows(step + 1, 1 - slot)
        for k in range(slot * CHUNK, (slot + 1) * CHUNK, batch):
            rows = [sticks[k + j : k + j + 1, :] for j in range(batch)]
            for j in range(batch):
                grid_rows[pl.ds(index[k + j], 1), :] = rows[j]

    walk(index_hbm, index, index_sem, scatter)

    def to_planes(u, _):
        turned = grid_rows[pl.ds(u * freqs, freqs), :].T
        for k in range(flat.shape[0]):
            upper = min(freqs - k * LANES, LANES)
            flat[k, pl.ds(u * ROWS, ROWS), 0:upper] = turned[0:ROWS, k * LANES : k * LANES + upper]
        return 0

    lax.fori_loop(0, freqs, to_planes, 0, unroll=8)
    position = lax.axis_index("fft")
    mine = columns[pl.ds(position * 2, 2), :]
    mine = jnp.concatenate([mine[0:1], mine[1:2]], axis=1)
    centre = freqs // 2
    along_u = jnp.floor((mine.astype(jnp.float32) + 0.5) * (1.0 / freqs)).astype(jnp.int32)
    along_v = mine - along_u * freqs - centre
    along_u = along_u - centre
    along_w = lax.broadcasted_iota(jnp.int32, (freqs, mine.shape[1]), 0) - centre
    squared = along_w * along_w + (along_u * along_u + along_v * along_v)
    kinetic[...] = squared.astype(jnp.float32) * (0.5 / float(centre * centre))


def place_call(recv, index, columns, freqs):
    tiles = -(-freqs // LANES)
    vmem = pl.BlockSpec(memory_space=pltpu.VMEM)
    anywhere = pl.BlockSpec(memory_space=pl.ANY)
    return pl.pallas_call(
        place_kernel,
        out_shape=(
            jax.ShapeDtypeStruct((tiles, freqs * ROWS, LANES), jnp.float32),
            jax.ShapeDtypeStruct((freqs, 2 * LANES), jnp.float32),
        ),
        in_specs=[anywhere, vmem, vmem],
        out_specs=(vmem, vmem),
        scratch_shapes=[
            pltpu.VMEM((2 * CHUNK, LANES), jnp.float32),
            pltpu.VMEM((freqs * freqs, LANES), jnp.float32),
            pltpu.SMEM((2 * CHUNK,), jnp.int32),
            pltpu.SemaphoreType.DMA((2,)),
        ],
        compiler_params=pltpu.CompilerParams(vmem_limit_bytes=60 * 1024 * 1024),
        name="place",
    )(index, columns.reshape(-1, LANES), recv)


def greet(position, count, own=None, bands=1, hops=()):
    barrier = pltpu.get_barrier_semaphore()
    for k in hops:
        pl.semaphore_signal(barrier, inc=1, device_id={"band": lax.rem(own + k, bands)}, device_id_type=MESH)

    def signal(k, _):
        pl.semaphore_signal(barrier, inc=1, device_id={"fft": lax.rem(position + k, count)}, device_id_type=MESH)
        return 0

    lax.fori_loop(1, count, signal, 0)
    return barrier


def await_others(buffer, semaphore):
    others = buffer.at[pl.ds(0, buffer.shape[0] - 1)]
    pltpu.make_async_copy(others, others, semaphore).wait()


def spread_kernel(
    psi_hbm,
    high_hbm,
    low_hbm,
    recv,
    psi,
    table_high,
    table_low,
    staged,
    send,
    load_sem,
    send_sem,
    recv_sem,
):
    count, pieces, depth, _ = recv.shape
    values = pieces * depth // 2
    position = lax.axis_index("fft")
    loads = start_loads(((psi_hbm, psi), (high_hbm, table_high), (low_hbm, table_low)), load_sem)
    barrier = greet(position, count)
    for load in loads:
        load.wait()
    high, low = split(psi[...])
    staged[...] = dot(table_high[...], high) + dot(table_low[...], high) + dot(table_high[...], low)
    pl.semaphore_wait(barrier, count - 1)

    def stage(peer):
        rows = staged[pl.ds(peer * ROWS, ROWS), :]
        block = jnp.concatenate([rows[:values, :LANES], rows[:values, LANES:]], axis=0)
        return [block[k * depth : (k + 1) * depth] for k in range(pieces)]

    def post(k, _):
        peer = lax.rem(position + k, count)
        for at, piece in enumerate(stage(peer)):
            send[peer, at] = piece
        pltpu.make_async_remote_copy(
            src_ref=send.at[peer],
            dst_ref=recv.at[position],
            send_sem=send_sem,
            recv_sem=recv_sem,
            device_id={"fft": peer},
            device_id_type=MESH,
        ).start()
        return 0

    lax.fori_loop(1, count, post, 0)
    for at, piece in enumerate(stage(position)):
        recv[position, at] = piece
    await_others(recv, recv_sem)
    await_others(recv, send_sem)


def spread_call(psi, table, count, planes_held):
    rows = table.shape[0]
    vmem = pl.BlockSpec(memory_space=pltpu.VMEM)
    shape = (count, planes_held, 2 * psi.shape[1] // LANES, LANES)
    return pl.pallas_call(
        spread_kernel,
        out_shape=jax.ShapeDtypeStruct(shape, jnp.float32),
        in_specs=[pl.BlockSpec(memory_space=pl.ANY)] * 3,
        out_specs=vmem,
        scratch_shapes=[
            pltpu.VMEM(psi.shape, jnp.float32),
            pltpu.VMEM(table.shape, jnp.bfloat16),
            pltpu.VMEM(table.shape, jnp.bfloat16),
            pltpu.VMEM((rows, psi.shape[1]), jnp.float32),
            pltpu.VMEM(shape, jnp.float32),
            pltpu.SemaphoreType.DMA((3,)),
            pltpu.SemaphoreType.DMA,
            pltpu.SemaphoreType.DMA,
        ],
        compiler_params=pltpu.CompilerParams(
            collective_id=0, has_side_effects=True, vmem_limit_bytes=60 * 1024 * 1024
        ),
        name="spread",
    )(psi, *halves(table))


def collect_kernel(
    scale,
    weight,
    index_hbm,
    within,
    psi_hbm,
    flat_hbm,
    potential_hbm,
    high_hbm,
    low_hbm,
    y_out_hbm,
    x_out_hbm,
    x_back_hbm,
    y_back_hbm,
    kinetic_hbm,
    local,
    margin,
    psi,
    flat,
    potential,
    table_high,
    table_low,
    y_out,
    x_out,
    x_back,
    y_back,
    kinetic,
    others,
    far,
    planes,
    grid_rows,
    sticks,
    send,
    got,
    right,
    sums,
    index,
    index_sem,
    load_sem,
    band_send_sem,
    band_recv_sem,
    far_send_sem,
    far_recv_sem,
    send_sem,
    recv_sem,
    sum_send_sem,
    sum_recv_sem,
):
    bands = others.shape[0] + 2
    hops = (1, bands - 1)
    count, pieces, depth, _ = got.shape
    values = pieces * depth // 2
    freqs = local.shape[2]
    per_device = local.shape[3]
    batch = 64
    position = lax.axis_index("fft")
    own = lax.axis_index("band")
    loads = start_loads(
        (
            (flat_hbm, flat),
            (y_out_hbm, y_out),
            (x_out_hbm, x_out),
            (potential_hbm, potential),
            (x_back_hbm, x_back),
            (y_back_hbm, y_back),
            (psi_hbm, psi),
            (high_hbm, table_high),
            (low_hbm, table_low),
            (kinetic_hbm, kinetic),
        ),
        load_sem,
    )
    barrier = greet(position, count, own, bands, hops)
    pl.semaphore_wait(barrier, count - 1 + len(hops))
    band_copies = [
        pltpu.make_async_remote_copy(
            src_ref=psi_hbm,
            dst_ref=others.at[at],
            send_sem=band_send_sem.at[at],
            recv_sem=band_recv_sem.at[at],
            device_id={"band": lax.rem(own + bands - k, bands)},
            device_id_type=MESH,
        )
        for at, k in enumerate(hops)
    ]
    for copy in band_copies:
        copy.start()
    for load in loads:
        load.wait()
    through_planes(flat, planes, potential, y_out, x_out, x_back, y_back)
    for copy in band_copies:
        copy.wait()
    far_copies = [
        pltpu.make_async_remote_copy(
            src_ref=others.at[at, pl.ds(at * freqs, freqs)],
            dst_ref=far.at[pl.ds(at * freqs, freqs)],
            send_sem=far_send_sem.at[at],
            recv_sem=far_recv_sem.at[at],
            device_id={"band": lax.rem(own + bands - k, bands)},
            device_id_type=MESH,
        )
        for at, k in enumerate(hops)
    ]
    for copy in far_copies:
        copy.start()

    def from_planes(i, _):
        for k in range(planes.shape[0]):
            upper = min(freqs - k * LANES, LANES)
            rows = [planes[k, pl.ds(i * PACK + j, ROWS, stride=freqs), :] for j in range(PACK)]
            rows = jnp.concatenate(rows, axis=0).T
            grid_rows[pl.ds(i * freqs + k * LANES, upper), 0 : PACK * ROWS] = rows[:upper]
        return 0

    lax.fori_loop(0, freqs // PACK, from_planes, 0, unroll=4)
    group = CHUNK // per_device
    steps = count // group
    first = lax.div(position, group) + 1
    sticks[CHUNK : 2 * CHUNK, :] = jnp.zeros((CHUNK, LANES), jnp.float32)

    def turned(at, line):
        rows = sticks[at : at + LANES, :].T
        place = within[pl.ds(line, 1), :]
        total = jnp.zeros((ROWS, LANES), jnp.float32)
        for k in range(PACK):
            total = jnp.where(place == k, rows[k * ROWS : (k + 1) * ROWS], total)
        return total[:values]

    def turn(step, slot):
        for k in range(group):
            peer = lax.rem(first + step, steps) * group + k
            at = slot * CHUNK + k * per_device
            block = jnp.concatenate([turned(at, peer * 2), turned(at + LANES, peer * 2 + 1)], axis=0)
            for piece in range(pieces):
                send[peer, piece] = block[piece * depth : (piece + 1) * depth]

    def post(step):
        for k in range(group):
            peer = lax.rem(first + step, steps) * group + k

            @pl.when(peer != position)
            def _(peer=peer):
                pltpu.make_async_remote_copy(
                    src_ref=send.at[peer],
                    dst_ref=got.at[position],
                    send_sem=send_sem,
                    recv_sem=recv_sem,
                    device_id={"fft": peer},
                    device_id_type=MESH,
                ).start()

    def gather(step, slot):
        for k in range(slot * CHUNK, (slot + 1) * CHUNK, batch):
            rows = [grid_rows[pl.ds(index[k + j], 1), :] for j in range(batch)]
            for j in range(batch):
                sticks[k + j : k + j + 1, :] = rows[j]
        turn(step + steps - 1, 1 - slot)

        @pl.when(step > 0)
        def _():
            post(step + steps - 1)

    walk(index_hbm, index, index_sem, gather, first)
    turn(steps - 1, 1)
    post(steps - 1)
    got[position] = send[position]
    await_others(got, recv_sem)

    def to_right(i, _):
        block = jnp.concatenate([got[i, k] for k in range(pieces)], axis=0)
        blank = jnp.zeros((ROWS - values, LANES), jnp.float32)
        at = pl.multiple_of(i * ROWS, ROWS)
        right[pl.ds(at, ROWS), 0:LANES] = jnp.concatenate([block[:values], blank], axis=0)
        right[pl.ds(at, ROWS), LANES : 2 * LANES] = jnp.concatenate([block[values:], blank], axis=0)
        return 0

    lax.fori_loop(0, count, to_right, 0, unroll=4)
    high, low = split(right[...])
    applied = dot(table_high[...], high) + dot(table_low[...], high) + dot(table_high[...], low)
    applied = applied * scale
    local[0, 0] = applied[:freqs]
    local[1, 0] = applied[freqs:]
    right_re = kinetic[...] * psi[0:freqs, :] + applied[:freqs]
    right_im = kinetic[...] * psi[freqs : 2 * freqs, :] + applied[freqs:]

    def folded(product):
        narrow = product[:, :LANES] + product[:, LANES:]
        return jnp.sum(narrow, axis=0, keepdims=True)

    for copy in far_copies:
        copy.wait()
    line = lax.broadcasted_iota(jnp.int32, (2 * bands, LANES), 0)
    tile = jnp.zeros((2 * bands, LANES), jnp.float32)
    for k in range(bands):
        left = psi if k == 0 else others.at[hops.index(k)] if k in hops else far
        left_re, left_im = left[0:freqs, :], left[freqs : 2 * freqs, :]
        row = lax.rem(own + k, bands)
        tile = jnp.where(line == row, folded(left_re * right_re + left_im * right_im), tile)
        tile = jnp.where(line == row + bands, folded(left_re * right_im - left_im * right_re), tile)
    sums[position] = tile * weight

    def post_sums(k, _):
        pltpu.make_async_remote_copy(
            src_ref=sums.at[position],
            dst_ref=sums.at[position],
            send_sem=sum_send_sem,
            recv_sem=sum_recv_sem,
            device_id={"fft": lax.rem(position + k, count)},
            device_id_type=MESH,
        ).start()
        return 0

    lax.fori_loop(1, count, post_sums, 0)
    await_others(sums, sum_recv_sem)
    result = jnp.sum(jnp.sum(sums[...], axis=0).T, axis=0, keepdims=True)
    margin[0] = result[:, :bands]
    margin[1] = result[:, bands:]
    await_others(got, send_sem)
    await_others(sums, sum_send_sem)


def collect_call(flat, kinetic, potential, index, within, psi, table, cosine, sine, scale, weight, shape, count, bands):
    freqs = cosine.shape[1]
    planes_held = potential.shape[0]
    vmem = pl.BlockSpec(memory_space=pltpu.VMEM)
    anywhere = pl.BlockSpec(memory_space=pl.ANY)
    table = table.T
    tables = plane_tables(cosine, sine)
    blocks = (count, planes_held, 2 * psi.shape[1] // LANES, LANES)
    operands = (psi, flat, potential, *halves(table), *tables, kinetic)
    return pl.pallas_call(
        functools.partial(collect_kernel, scale, weight),
        out_shape=(jax.ShapeDtypeStruct(shape, jnp.float32), jax.ShapeDtypeStruct((2, 1, bands), jnp.float32)),
        in_specs=[anywhere, vmem] + [anywhere] * len(operands),
        out_specs=(vmem, vmem),
        scratch_shapes=[
            *[pltpu.VMEM(operand.shape, operand.dtype) for operand in operands],
            pltpu.VMEM((2, *psi.shape), jnp.float32),
            pltpu.VMEM(psi.shape, jnp.float32),
            pltpu.VMEM((flat.shape[0], ROWS * freqs, LANES), jnp.float32),
            pltpu.VMEM((freqs // PACK * freqs, LANES), jnp.float32),
            pltpu.VMEM((2 * CHUNK, LANES), jnp.float32),
            pltpu.VMEM(blocks, jnp.float32),
            pltpu.VMEM(blocks, jnp.float32),
            pltpu.VMEM((count * ROWS, psi.shape[1]), jnp.float32),
            pltpu.VMEM((count, 2 * bands, LANES), jnp.float32),
            pltpu.SMEM((2 * CHUNK,), jnp.int32),
            pltpu.SemaphoreType.DMA((2,)),
            pltpu.SemaphoreType.DMA((len(operands),)),
            pltpu.SemaphoreType.DMA((2,)),
            pltpu.SemaphoreType.DMA((2,)),
            pltpu.SemaphoreType.DMA((2,)),
            pltpu.SemaphoreType.DMA((2,)),
            pltpu.SemaphoreType.DMA,
            pltpu.SemaphoreType.DMA,
            pltpu.SemaphoreType.DMA,
            pltpu.SemaphoreType.DMA,
        ],
        compiler_params=pltpu.CompilerParams(
            collective_id=1, has_side_effects=True, vmem_limit_bytes=60 * 1024 * 1024
        ),
        name="collect",
    )(index, within.reshape(-1, LANES), *operands)


def on_device(psi, potential, stick_columns):
    freq_count = psi.shape[2]
    per_device = psi.shape[3]
    grid_size = potential.shape[1]
    plane_count = potential.shape[0]
    fft_count = lax.axis_size("fft")
    cosine, sine = dft_tables(grid_size, freq_count)
    table = np.stack([np.concatenate([cosine, -sine], 1), np.concatenate([sine, cosine], 1)])
    table = table.reshape(2, fft_count, plane_count, 2 * freq_count).transpose(1, 0, 2, 3)
    table = table.reshape(fft_count, 2 * plane_count, 2 * freq_count)
    table = np.pad(table, ((0, 0), (0, ROWS - 2 * plane_count), (0, 0))).reshape(fft_count * ROWS, 2 * freq_count)
    flat_psi = psi.reshape(2 * freq_count, per_device)
    moved = spread_call(flat_psi, table, fft_count, plane_count)
    bands = lax.axis_size("band")
    if freq_count == 160:
        fives = lax.shift_right_logical(stick_columns, 5)
        along_u = lax.shift_right_logical(fives * 52429, 18)
    else:
        along_u = stick_columns // freq_count
    along_v = stick_columns - along_u * freq_count
    along_u = (along_u & 1) * (freq_count // 2) + lax.shift_right_logical(along_u, 1)
    out_index = along_u * freq_count + along_v
    back_index = lax.shift_right_logical(along_u, PACK.bit_length() - 1) * freq_count + along_v
    flat, kinetic = place_call(moved, out_index, stick_columns, freq_count)
    scale = 1.0 / float(grid_size * grid_size * grid_size)
    weight = 1.0 / float(freq_count * per_device * fft_count)
    applied, margin = collect_call(
        flat,
        kinetic,
        potential,
        back_index,
        along_u & (PACK - 1),
        flat_psi,
        table,
        cosine,
        sine,
        scale,
        weight,
        psi.shape,
        fft_count,
        bands,
    )
    return (kinetic * psi + applied, margin.swapaxes(1, 2))


def solution(mesh):
    placed = (P(None, "band", None, "fft"), P("fft", None, None), P())
    return jax.shard_map(
        on_device,
        mesh=mesh,
        in_specs=placed,
        out_specs=(P(None, "band", None, "fft"), P(None, None, "band")),
        check_vma=False,
    )
```

```python
import functools
import math

import jax
import jax.numpy as jnp
import numpy as np
from jax import lax
from jax.experimental import pallas as pl
from jax.experimental.pallas import tpu as pltpu
from jax.sharding import PartitionSpec as P

LANES = 128
ROWS = 16
PACK = 4
CHUNK = 1024
MESH = pl.DeviceIdType.MESH


def dft_tables(grid_size, freq_count):
    points = np.arange(grid_size)[:, None]
    freqs = np.arange(freq_count)[None, :] - freq_count // 2
    angle = (points * freqs % grid_size).astype(np.float64) * (2.0 * math.pi / grid_size)
    return np.cos(angle).astype(np.float32), np.sin(angle).astype(np.float32)


def halves(table):
    high = table.astype(jnp.bfloat16)
    low = (table - high.astype(np.float32)).astype(jnp.bfloat16)
    return high, low


def split(value):
    high = value.astype(jnp.bfloat16)
    low = (value - high.astype(jnp.float32)).astype(jnp.bfloat16)
    return high, low


def dot(left, right):
    return jnp.dot(left, right, preferred_element_type=jnp.float32)


def packed_rows(table, whole):
    high, low = halves(table)
    tail = table.shape[0] - whole
    spare = np.zeros((-3 * tail % LANES, table.shape[1]), high.dtype)
    if whole % (2 * LANES) == 0:
        spare = np.zeros((-3 * tail % (2 * LANES), table.shape[1]), high.dtype)
    return np.concatenate([high[:whole], high[:whole], low[:whole], high[whole:], high[whole:], low[whole:], spare], axis=0)


def packed_columns(value, whole, tail):
    high, low = split(value)
    rest_high = high[:, whole : whole + LANES].astype(jnp.float32)
    rest_low = low[:, whole : whole + LANES].astype(jnp.float32)
    parts = [high[:, :whole], low[:, :whole], high[:, :whole]]
    if 3 * tail <= LANES:
        rest = rest_high + pltpu.roll(rest_low, tail, 1) + pltpu.roll(rest_high, 2 * tail, 1)
        parts.append(rest.astype(jnp.bfloat16))
    else:
        parts.append((rest_high + pltpu.roll(rest_low, tail, 1)).astype(jnp.bfloat16))
        parts.append(rest_high.astype(jnp.bfloat16))
    return jnp.concatenate(parts, axis=1)


def three(table):
    high, low = halves(table)
    return np.concatenate([high, low, high], axis=1)


def whole_lanes(count):
    return count // LANES * LANES


def plane_tables(cosine, sine):
    grid, freqs = cosine.shape
    half = grid // 2
    wide = -(-grid // LANES) * LANES
    wide_v = -(-freqs // LANES) * LANES
    y_out = np.zeros((freqs, 2 * wide), np.float32)
    y_out[:, :grid] = cosine.T
    y_out[:, wide : wide + grid] = sine.T
    y_back = np.zeros((grid, 2 * wide_v), np.float32)
    y_back[:, :freqs] = cosine
    y_back[:, wide_v : wide_v + freqs] = sine
    x_out = [three(np.concatenate([cosine[:half, k::2], sine[:half, k::2]], axis=0)) for k in (0, 1)]
    x_back = [three(np.concatenate([cosine[:half, k::2].T, sine[:half, k::2].T], axis=0)) for k in (0, 1)]
    return (
        packed_rows(y_out, whole_lanes(freqs)),
        np.stack(x_out),
        np.stack(x_back),
        packed_rows(y_back, whole_lanes(grid)),
    )


def stacked(value):
    high, low = split(value)
    return jnp.concatenate([high, high, low], axis=0)


def complex_parts(prod, rows, wide, sign):
    real = prod[:rows, :wide] - sign * prod[rows:, wide:]
    imag = prod[:rows, wide:] + sign * prod[rows:, :wide]
    return real, imag


def walk(columns, index, index_sem, visit, first=0):
    steps = columns.shape[0] // CHUNK

    def number_of(step):
        return lax.rem(first + step, steps)

    def fetch(step, slot):
        source = columns.at[pl.ds(pl.multiple_of(number_of(step) * CHUNK, CHUNK), CHUNK)]
        return pltpu.make_async_copy(source, index.at[pl.ds(slot * CHUNK, CHUNK)], index_sem.at[slot])

    fetch(0, 0).start()

    def pair(i, _):
        fetch(2 * i + 1, 1).start()
        fetch(2 * i, 0).wait()
        visit(2 * i, 0)

        @pl.when(i < steps // 2 - 1)
        def _():
            fetch(2 * i + 2, 0).start()

        fetch(2 * i + 1, 1).wait()
        visit(2 * i + 1, 1)
        return 0

    lax.fori_loop(0, steps // 2, pair, 0)


def through_planes(flat, planes, potential, y_out, x_out, x_back, y_back):
    planes_held, grid, _ = potential.shape
    half = grid // 2
    freqs = x_back.shape[1]
    even = freqs // 2
    wide = y_out.shape[1] // 2
    wide_v = y_back.shape[1] // 2

    def plane(z, _):
        lane = lax.broadcasted_iota(jnp.int32, (2 * freqs, LANES), 1)
        tiles = []
        for k in range(flat.shape[0]):
            pair = [flat[k, pl.ds(at, freqs, stride=ROWS), :] for at in (z, planes_held + z)]
            pair = jnp.concatenate(pair, axis=0)
            tiles.append(pair if freqs - k * LANES >= LANES else jnp.where(lane < freqs - k * LANES, pair, 0.0))
        left = packed_columns(jnp.concatenate(tiles, axis=1), whole_lanes(freqs), freqs % LANES)
        along = jnp.concatenate(complex_parts(dot(left, y_out[...]), freqs, wide, 1.0), axis=1)
        first_re, first_im = complex_parts(dot(x_out[0], stacked(along[:even])), half, wide, 1.0)
        second_re, second_im = complex_parts(dot(x_out[1], stacked(along[even:])), half, wide, 1.0)
        lower = potential[z, 0:half, :]
        upper = potential[z, half:grid, :]
        blank = jnp.zeros((half, wide - grid), jnp.float32)
        lower = jnp.concatenate([lower, blank], axis=1)
        upper = jnp.concatenate([upper, blank], axis=1)
        low_re, low_im = (first_re + second_re) * lower, (first_im + second_im) * lower
        up_re, up_im = (first_re - second_re) * upper, (first_im - second_im) * upper
        added = jnp.concatenate([low_re + up_re, low_im + up_im], axis=1)
        taken = jnp.concatenate([low_re - up_re, low_im - up_im], axis=1)
        even_re, even_im = complex_parts(dot(x_back[0], stacked(added)), even, wide, -1.0)
        odd_re, odd_im = complex_parts(dot(x_back[1], stacked(taken)), even, wide, -1.0)
        left = packed_columns(
            jnp.concatenate([even_re, odd_re, even_im, odd_im], axis=0), whole_lanes(grid), grid % LANES
        )
        prod = dot(left, y_back[...])
        done_re = prod[:freqs, :wide_v] + prod[freqs:, wide_v:]
        done_im = prod[freqs:, :wide_v] - prod[:freqs, wide_v:]
        for k in range(planes.shape[0]):
            planes[k, pl.ds(z * freqs, freqs), :] = done_re[:, k * LANES : (k + 1) * LANES]
            planes[k, pl.ds((planes_held + z) * freqs, freqs), :] = done_im[:, k * LANES : (k + 1) * LANES]
        return 0

    lax.fori_loop(0, planes_held, plane, 0)


def start_loads(pairs, semaphore):
    loads = [pltpu.make_async_copy(source, target, semaphore.at[k]) for k, (source, target) in enumerate(pairs)]
    for load in loads:
        load.start()
    return loads


def place_kernel(index_hbm, columns, recv, flat, kinetic, sticks, grid_rows, index, index_sem):
    blocks, pieces, depth, _ = recv.shape
    values = pieces * depth // 2
    freqs = flat.shape[1] // ROWS
    batch = 64

    def clear(i, _):
        grid_rows[pl.ds(i * freqs, freqs), :] = jnp.zeros((freqs, LANES), jnp.float32)
        return 0

    lax.fori_loop(0, freqs, clear, 0)

    per_device = 2 * LANES
    group = CHUNK // per_device
    steps = blocks // group

    def to_rows(step, slot):
        for b in range(group):
            i = lax.rem(step, steps) * group + b
            block = jnp.concatenate([recv[i, k] for k in range(pieces)], axis=0)
            block = jnp.concatenate([block, jnp.zeros((LANES - block.shape[0], LANES), jnp.float32)], axis=0)
            turned = block.T
            at = slot * CHUNK + b * per_device
            sticks[at : at + LANES, :] = turned
            sticks[at + LANES : at + per_device, :] = pltpu.roll(turned, LANES - values, 1)

    to_rows(0, 0)

    def scatter(step, slot):
        to_rows(step + 1, 1 - slot)
        for k in range(slot * CHUNK, (slot + 1) * CHUNK, batch):
            rows = [sticks[k + j : k + j + 1, :] for j in range(batch)]
            for j in range(batch):
                grid_rows[pl.ds(index[k + j], 1), :] = rows[j]

    walk(index_hbm, index, index_sem, scatter)

    def to_planes(u, _):
        turned = grid_rows[pl.ds(u * freqs, freqs), :].T
        for k in range(flat.shape[0]):
            upper = min(freqs - k * LANES, LANES)
            flat[k, pl.ds(u * ROWS, ROWS), 0:upper] = turned[0:ROWS, k * LANES : k * LANES + upper]
        return 0

    lax.fori_loop(0, freqs, to_planes, 0, unroll=8)
    position = lax.axis_index("fft")
    mine = columns[pl.ds(position * 2, 2), :]
    mine = jnp.concatenate([mine[0:1], mine[1:2]], axis=1)
    centre = freqs // 2
    along_u = jnp.floor((mine.astype(jnp.float32) + 0.5) * (1.0 / freqs)).astype(jnp.int32)
    along_v = mine - along_u * freqs - centre
    along_u = along_u - centre
    along_w = lax.broadcasted_iota(jnp.int32, (freqs, mine.shape[1]), 0) - centre
    squared = along_w * along_w + (along_u * along_u + along_v * along_v)
    kinetic[...] = squared.astype(jnp.float32) * (0.5 / float(centre * centre))


def place_call(recv, index, columns, freqs):
    tiles = -(-freqs // LANES)
    vmem = pl.BlockSpec(memory_space=pltpu.VMEM)
    anywhere = pl.BlockSpec(memory_space=pl.ANY)
    return pl.pallas_call(
        place_kernel,
        out_shape=(
            jax.ShapeDtypeStruct((tiles, freqs * ROWS, LANES), jnp.float32),
            jax.ShapeDtypeStruct((freqs, 2 * LANES), jnp.float32),
        ),
        in_specs=[anywhere, vmem, vmem],
        out_specs=(vmem, vmem),
        scratch_shapes=[
            pltpu.VMEM((2 * CHUNK, LANES), jnp.float32),
            pltpu.VMEM((freqs * freqs, LANES), jnp.float32),
            pltpu.SMEM((2 * CHUNK,), jnp.int32),
            pltpu.SemaphoreType.DMA((2,)),
        ],
        compiler_params=pltpu.CompilerParams(vmem_limit_bytes=60 * 1024 * 1024),
        name="place",
    )(index, columns.reshape(-1, LANES), recv)


def greet(position, count, own=None, bands=1, hops=()):
    barrier = pltpu.get_barrier_semaphore()
    for k in hops:
        pl.semaphore_signal(barrier, inc=1, device_id={"band": lax.rem(own + k, bands)}, device_id_type=MESH)

    def signal(k, _):
        pl.semaphore_signal(barrier, inc=1, device_id={"fft": lax.rem(position + k, count)}, device_id_type=MESH)
        return 0

    lax.fori_loop(1, count, signal, 0)
    return barrier


def await_others(buffer, semaphore):
    others = buffer.at[pl.ds(0, buffer.shape[0] - 1)]
    pltpu.make_async_copy(others, others, semaphore).wait()


def spread_kernel(
    psi_hbm,
    high_hbm,
    low_hbm,
    recv,
    psi,
    table_high,
    table_low,
    staged,
    send,
    load_sem,
    send_sem,
    recv_sem,
):
    count, pieces, depth, _ = recv.shape
    values = pieces * depth // 2
    position = lax.axis_index("fft")
    loads = start_loads(((psi_hbm, psi), (high_hbm, table_high), (low_hbm, table_low)), load_sem)
    barrier = greet(position, count)
    for load in loads:
        load.wait()
    high, low = split(psi[...])
    staged[...] = dot(table_high[...], high) + dot(table_low[...], high) + dot(table_high[...], low)
    pl.semaphore_wait(barrier, count - 1)

    def stage(peer):
        rows = staged[pl.ds(peer * ROWS, ROWS), :]
        block = jnp.concatenate([rows[:values, :LANES], rows[:values, LANES:]], axis=0)
        return [block[k * depth : (k + 1) * depth] for k in range(pieces)]

    def post(k, _):
        peer = lax.rem(position + k, count)
        for at, piece in enumerate(stage(peer)):
            send[peer, at] = piece
        pltpu.make_async_remote_copy(
            src_ref=send.at[peer],
            dst_ref=recv.at[position],
            send_sem=send_sem,
            recv_sem=recv_sem,
            device_id={"fft": peer},
            device_id_type=MESH,
        ).start()
        return 0

    lax.fori_loop(1, count, post, 0)
    for at, piece in enumerate(stage(position)):
        recv[position, at] = piece
    await_others(recv, recv_sem)
    await_others(recv, send_sem)


def spread_call(psi, table, count, planes_held):
    rows = table.shape[0]
    vmem = pl.BlockSpec(memory_space=pltpu.VMEM)
    shape = (count, planes_held, 2 * psi.shape[1] // LANES, LANES)
    return pl.pallas_call(
        spread_kernel,
        out_shape=jax.ShapeDtypeStruct(shape, jnp.float32),
        in_specs=[pl.BlockSpec(memory_space=pl.ANY)] * 3,
        out_specs=vmem,
        scratch_shapes=[
            pltpu.VMEM(psi.shape, jnp.float32),
            pltpu.VMEM(table.shape, jnp.bfloat16),
            pltpu.VMEM(table.shape, jnp.bfloat16),
            pltpu.VMEM((rows, psi.shape[1]), jnp.float32),
            pltpu.VMEM(shape, jnp.float32),
            pltpu.SemaphoreType.DMA((3,)),
            pltpu.SemaphoreType.DMA,
            pltpu.SemaphoreType.DMA,
        ],
        compiler_params=pltpu.CompilerParams(
            collective_id=0, has_side_effects=True, vmem_limit_bytes=60 * 1024 * 1024
        ),
        name="spread",
    )(psi, *halves(table))


def collect_kernel(
    scale,
    weight,
    index_hbm,
    within,
    psi_hbm,
    flat_hbm,
    potential_hbm,
    high_hbm,
    low_hbm,
    y_out_hbm,
    x_out_hbm,
    x_back_hbm,
    y_back_hbm,
    kinetic_hbm,
    local,
    margin,
    psi,
    flat,
    potential,
    table_high,
    table_low,
    y_out,
    x_out,
    x_back,
    y_back,
    kinetic,
    others,
    far,
    planes,
    grid_rows,
    sticks,
    send,
    got,
    right,
    sums,
    index,
    index_sem,
    load_sem,
    band_send_sem,
    band_recv_sem,
    far_send_sem,
    far_recv_sem,
    send_sem,
    recv_sem,
    sum_send_sem,
    sum_recv_sem,
):
    bands = others.shape[0] + 2
    hops = (1, bands - 1)
    count, pieces, depth, _ = got.shape
    values = pieces * depth // 2
    freqs = local.shape[2]
    per_device = local.shape[3]
    batch = 64
    position = lax.axis_index("fft")
    own = lax.axis_index("band")
    loads = start_loads(
        (
            (flat_hbm, flat),
            (y_out_hbm, y_out),
            (x_out_hbm, x_out),
            (potential_hbm, potential),
            (x_back_hbm, x_back),
            (y_back_hbm, y_back),
            (psi_hbm, psi),
            (high_hbm, table_high),
            (low_hbm, table_low),
            (kinetic_hbm, kinetic),
        ),
        load_sem,
    )
    barrier = greet(position, count, own, bands, hops)
    pl.semaphore_wait(barrier, count - 1 + len(hops))
    band_copies = [
        pltpu.make_async_remote_copy(
            src_ref=psi_hbm,
            dst_ref=others.at[at],
            send_sem=band_send_sem.at[at],
            recv_sem=band_recv_sem.at[at],
            device_id={"band": lax.rem(own + bands - k, bands)},
            device_id_type=MESH,
        )
        for at, k in enumerate(hops)
    ]
    for copy in band_copies:
        copy.start()
    for load in loads:
        load.wait()
    through_planes(flat, planes, potential, y_out, x_out, x_back, y_back)

    def from_planes(i, _):
        for k in range(planes.shape[0]):
            upper = min(freqs - k * LANES, LANES)
            rows = [planes[k, pl.ds(i * PACK + j, ROWS, stride=freqs), :] for j in range(PACK)]
            rows = jnp.concatenate(rows, axis=0).T
            grid_rows[pl.ds(i * freqs + k * LANES, upper), 0 : PACK * ROWS] = rows[:upper]
        return 0

    lax.fori_loop(0, freqs // PACK, from_planes, 0, unroll=4)
    group = CHUNK // per_device
    steps = count // group
    first = lax.div(position, group) + 1
    sticks[CHUNK : 2 * CHUNK, :] = jnp.zeros((CHUNK, LANES), jnp.float32)

    def turned(at, line):
        rows = sticks[at : at + LANES, :].T
        place = within[pl.ds(line, 1), :]
        total = jnp.zeros((ROWS, LANES), jnp.float32)
        for k in range(PACK):
            total = jnp.where(place == k, rows[k * ROWS : (k + 1) * ROWS], total)
        return total[:values]

    def turn(step, slot):
        for k in range(group):
            peer = lax.rem(first + step, steps) * group + k
            at = slot * CHUNK + k * per_device
            block = jnp.concatenate([turned(at, peer * 2), turned(at + LANES, peer * 2 + 1)], axis=0)
            for piece in range(pieces):
                send[peer, piece] = block[piece * depth : (piece + 1) * depth]

    def post(step):
        for k in range(group):
            peer = lax.rem(first + step, steps) * group + k

            @pl.when(peer != position)
            def _(peer=peer):
                pltpu.make_async_remote_copy(
                    src_ref=send.at[peer],
                    dst_ref=got.at[position],
                    send_sem=send_sem,
                    recv_sem=recv_sem,
                    device_id={"fft": peer},
                    device_id_type=MESH,
                ).start()

    def gather(step, slot):
        for k in range(slot * CHUNK, (slot + 1) * CHUNK, batch):
            rows = [grid_rows[pl.ds(index[k + j], 1), :] for j in range(batch)]
            for j in range(batch):
                sticks[k + j : k + j + 1, :] = rows[j]
        turn(step + steps - 1, 1 - slot)

        @pl.when(step > 0)
        def _():
            post(step + steps - 1)

    walk(index_hbm, index, index_sem, gather, first)
    turn(steps - 1, 1)
    post(steps - 1)
    for copy in band_copies:
        copy.wait()
    far_copies = [
        pltpu.make_async_remote_copy(
            src_ref=others.at[at, pl.ds(at * freqs, freqs)],
            dst_ref=far.at[pl.ds(at * freqs, freqs)],
            send_sem=far_send_sem.at[at],
            recv_sem=far_recv_sem.at[at],
            device_id={"band": lax.rem(own + bands - k, bands)},
            device_id_type=MESH,
        )
        for at, k in enumerate(hops)
    ]
    for copy in far_copies:
        copy.start()
    got[position] = send[position]
    await_others(got, recv_sem)

    def to_right(i, _):
        block = jnp.concatenate([got[i, k] for k in range(pieces)], axis=0)
        blank = jnp.zeros((ROWS - values, LANES), jnp.float32)
        at = pl.multiple_of(i * ROWS, ROWS)
        right[pl.ds(at, ROWS), 0:LANES] = jnp.concatenate([block[:values], blank], axis=0)
        right[pl.ds(at, ROWS), LANES : 2 * LANES] = jnp.concatenate([block[values:], blank], axis=0)
        return 0

    lax.fori_loop(0, count, to_right, 0, unroll=4)
    high, low = split(right[...])
    applied = dot(table_high[...], high) + dot(table_low[...], high) + dot(table_high[...], low)
    applied = applied * scale
    local[0, 0] = applied[:freqs]
    local[1, 0] = applied[freqs:]
    right_re = kinetic[...] * psi[0:freqs, :] + applied[:freqs]
    right_im = kinetic[...] * psi[freqs : 2 * freqs, :] + applied[freqs:]

    def folded(product):
        narrow = product[:, :LANES] + product[:, LANES:]
        return jnp.sum(narrow, axis=0, keepdims=True)

    for copy in far_copies:
        copy.wait()
    line = lax.broadcasted_iota(jnp.int32, (2 * bands, LANES), 0)
    tile = jnp.zeros((2 * bands, LANES), jnp.float32)
    for k in range(bands):
        left = psi if k == 0 else others.at[hops.index(k)] if k in hops else far
        left_re, left_im = left[0:freqs, :], left[freqs : 2 * freqs, :]
        row = lax.rem(own + k, bands)
        tile = jnp.where(line == row, folded(left_re * right_re + left_im * right_im), tile)
        tile = jnp.where(line == row + bands, folded(left_re * right_im - left_im * right_re), tile)
    sums[position] = tile * weight

    def post_sums(k, _):
        pltpu.make_async_remote_copy(
            src_ref=sums.at[position],
            dst_ref=sums.at[position],
            send_sem=sum_send_sem,
            recv_sem=sum_recv_sem,
            device_id={"fft": lax.rem(position + k, count)},
            device_id_type=MESH,
        ).start()
        return 0

    lax.fori_loop(1, count, post_sums, 0)
    await_others(sums, sum_recv_sem)
    result = jnp.sum(jnp.sum(sums[...], axis=0).T, axis=0, keepdims=True)
    margin[0] = result[:, :bands]
    margin[1] = result[:, bands:]
    await_others(got, send_sem)
    await_others(sums, sum_send_sem)


def collect_call(flat, kinetic, potential, index, within, psi, table, cosine, sine, scale, weight, shape, count, bands):
    freqs = cosine.shape[1]
    planes_held = potential.shape[0]
    vmem = pl.BlockSpec(memory_space=pltpu.VMEM)
    anywhere = pl.BlockSpec(memory_space=pl.ANY)
    table = table.T
    tables = plane_tables(cosine, sine)
    blocks = (count, planes_held, 2 * psi.shape[1] // LANES, LANES)
    operands = (psi, flat, potential, *halves(table), *tables, kinetic)
    return pl.pallas_call(
        functools.partial(collect_kernel, scale, weight),
        out_shape=(jax.ShapeDtypeStruct(shape, jnp.float32), jax.ShapeDtypeStruct((2, 1, bands), jnp.float32)),
        in_specs=[anywhere, vmem] + [anywhere] * len(operands),
        out_specs=(vmem, vmem),
        scratch_shapes=[
            *[pltpu.VMEM(operand.shape, operand.dtype) for operand in operands],
            pltpu.VMEM((2, *psi.shape), jnp.float32),
            pltpu.VMEM(psi.shape, jnp.float32),
            pltpu.VMEM((flat.shape[0], ROWS * freqs, LANES), jnp.float32),
            pltpu.VMEM((freqs // PACK * freqs, LANES), jnp.float32),
            pltpu.VMEM((2 * CHUNK, LANES), jnp.float32),
            pltpu.VMEM(blocks, jnp.float32),
            pltpu.VMEM(blocks, jnp.float32),
            pltpu.VMEM((count * ROWS, psi.shape[1]), jnp.float32),
            pltpu.VMEM((count, 2 * bands, LANES), jnp.float32),
            pltpu.SMEM((2 * CHUNK,), jnp.int32),
            pltpu.SemaphoreType.DMA((2,)),
            pltpu.SemaphoreType.DMA((len(operands),)),
            pltpu.SemaphoreType.DMA((2,)),
            pltpu.SemaphoreType.DMA((2,)),
            pltpu.SemaphoreType.DMA((2,)),
            pltpu.SemaphoreType.DMA((2,)),
            pltpu.SemaphoreType.DMA,
            pltpu.SemaphoreType.DMA,
            pltpu.SemaphoreType.DMA,
            pltpu.SemaphoreType.DMA,
        ],
        compiler_params=pltpu.CompilerParams(
            collective_id=1, has_side_effects=True, vmem_limit_bytes=60 * 1024 * 1024
        ),
        name="collect",
    )(index, within.reshape(-1, LANES), *operands)


def on_device(psi, potential, stick_columns):
    freq_count = psi.shape[2]
    per_device = psi.shape[3]
    grid_size = potential.shape[1]
    plane_count = potential.shape[0]
    fft_count = lax.axis_size("fft")
    cosine, sine = dft_tables(grid_size, freq_count)
    table = np.stack([np.concatenate([cosine, -sine], 1), np.concatenate([sine, cosine], 1)])
    table = table.reshape(2, fft_count, plane_count, 2 * freq_count).transpose(1, 0, 2, 3)
    table = table.reshape(fft_count, 2 * plane_count, 2 * freq_count)
    table = np.pad(table, ((0, 0), (0, ROWS - 2 * plane_count), (0, 0))).reshape(fft_count * ROWS, 2 * freq_count)
    flat_psi = psi.reshape(2 * freq_count, per_device)
    moved = spread_call(flat_psi, table, fft_count, plane_count)
    bands = lax.axis_size("band")
    if freq_count == 160:
        fives = lax.shift_right_logical(stick_columns, 5)
        along_u = lax.shift_right_logical(fives * 52429, 18)
    else:
        along_u = stick_columns // freq_count
    along_v = stick_columns - along_u * freq_count
    along_u = (along_u & 1) * (freq_count // 2) + lax.shift_right_logical(along_u, 1)
    out_index = along_u * freq_count + along_v
    back_index = lax.shift_right_logical(along_u, PACK.bit_length() - 1) * freq_count + along_v
    flat, kinetic = place_call(moved, out_index, stick_columns, freq_count)
    scale = 1.0 / float(grid_size * grid_size * grid_size)
    weight = 1.0 / float(freq_count * per_device * fft_count)
    applied, margin = collect_call(
        flat,
        kinetic,
        potential,
        back_index,
        along_u & (PACK - 1),
        flat_psi,
        table,
        cosine,
        sine,
        scale,
        weight,
        psi.shape,
        fft_count,
        bands,
    )
    return (kinetic * psi + applied, margin.swapaxes(1, 2))


def solution(mesh):
    placed = (P(None, "band", None, "fft"), P("fft", None, None), P())
    return jax.shard_map(
        on_device,
        mesh=mesh,
        in_specs=placed,
        out_specs=(P(None, "band", None, "fft"), P(None, None, "band")),
        check_vma=False,
    )
```
